128 devices in a mesh: row: 8 (over x, core), col: 16 (over y, z).
Axes of the slice: x: 4, y: 4, z: 4, core: 2. Of those that a mesh axis runs over, the one named last changes fastest.
Arguments:
- atom_feat: bfloat16 [16384, 128], P(('row', 'col')), may hold values from -6 to 6
- atom_token: int32 [16384], P(('row', 'col')), may hold values from 0 to 2047, as said below
- w_atom_qkv: bfloat16 [128, 384], replicated, may hold values from -0.5 to 0.5
- w_atom_out: bfloat16 [128, 128], replicated, may hold values from -0.5 to 0.5
- w_atom_up: bfloat16 [128, 768], replicated, may hold values from -0.5 to 0.5
- pair_repr: bfloat16 [2048, 8, 256, 128], P('row', None, 'col'), may hold values from -6 to 6
- w_bias: float32 [128, 16], replicated, may hold values from -16 to 16
- w_query: bfloat16 [768, 768], replicated, may hold values from -0.21875 to 0.21875
- w_kv: bfloat16 [768, 1536], replicated, may hold values from -0.21875 to 0.21875
- w_gate: bfloat16 [768, 768], replicated, may hold values from -0.21875 to 0.21875
- w_out: bfloat16 [768, 768], replicated, may hold values from -0.21875 to 0.21875
- w_down: bfloat16 [768, 128], replicated, may hold values from -0.21875 to 0.21875
Outputs:
- token_out: bfloat16 [2048, 768], P('row', 'col')
- atom_final: bfloat16 [16384, 128], P(('row', 'col'))
The draws below stay inside these ranges and needn't reach their ends.
Inputs may be any that keep to these rules, and one draw needn't show every extreme that they name: atom_token never falls along the atoms; the atoms held by the device with index r along row name only tokens r*256 to r*256 + 255, and every token is named by at least one atom.
All inputs are finite; a program needn't handle non-finite values.
Results may differ from the reference program's by a relative error of at most 0.017.
The reference program's roundings to bfloat16 on the way count: a program that leaves them out, or rounds other values in their place, can miss the bound.
Values may be sent and summed in bfloat16 or wider, within the bound.
A program may use at most 192 MiB of HBM per device.

```python
import jax
import jax.numpy as jnp
from jax import lax

D = 768
HEADS = 16
DH = 48
CP = 128
CA = 128
AHEADS = 4
ADH = 32
QBLOCK = 32
KWIN = 128
HALO = 48
TOK_ROW = 256
NTOK = 2048
ATOM_ROW = 2048
ATOMS = 16384
N_ROW = 8


def draw_atom_token(key, part):
    key = jax.random.fold_in(key, 11)
    first_key, second_key = jax.random.split(key)
    groups = NTOK // TOK_ROW
    extra = ATOM_ROW - TOK_ROW
    first = jax.random.randint(first_key, (groups, extra), 0, TOK_ROW)
    second = jax.random.randint(second_key, (groups, extra), 0, TOK_ROW)
    chosen = jnp.minimum(first, second)
    every = jnp.broadcast_to(jnp.arange(TOK_ROW, dtype=jnp.int32)[None, :], (groups, TOK_ROW))
    joined = jnp.sort(jnp.concatenate([every, chosen.astype(jnp.int32)], axis=1), axis=1)
    offset = (jnp.arange(groups, dtype=jnp.int32) * TOK_ROW)[:, None]
    return (joined + offset).reshape(-1).astype(jnp.int32)


def draw_w_bias(key, part):
    key = jax.random.fold_in(key, 12)
    base_key, scale_key = jax.random.split(key)
    values = jnp.clip(jax.random.normal(base_key, (CP, HEADS), jnp.float32), -3.0, 3.0) / CP ** 0.5
    scales = jnp.exp(jax.random.uniform(scale_key, (1, HEADS), jnp.float32, -0.7, 1.1))
    return jnp.clip(values * scales, -16.0, 16.0).astype(jnp.float32)


def level_of(key, shape, pieces, smallest, largest):
    loudness = 1.0
    for dim, blocks in pieces:
        draws = jax.random.uniform(jax.random.fold_in(jax.random.fold_in(key, 6), dim), (blocks,), jnp.float32, smallest / len(pieces), largest / len(pieces))
        loudness = loudness * jnp.repeat(jnp.exp(draws), shape[dim] // blocks).reshape((-1,) + (1,) * (len(shape) - 1 - dim))
    return loudness


def normal_values(rng, shape, scale, reach, cuts=(), held_as=jnp.bfloat16):
    factor_of = level_of(rng, shape, cuts, -0.22, 0.18) if cuts else 1.0
    result = jax.random.normal(rng, shape, jnp.float32) * scale * factor_of
    return jnp.minimum(jnp.maximum(result, -reach), reach).astype(held_as)


def setup_inputs(seed: int = 0) -> dict:
    splits = jax.random.split(jax.random.key(seed), 13)
    return {
        "atom_feat": normal_values(splits[0], (ATOMS, CA), 1.0, 6.0, ((0, 128),)),
        "atom_token": draw_atom_token(jax.random.fold_in(splits[12], 71), 0),
        "w_atom_qkv": normal_values(splits[2], (CA, 3 * CA), CA ** -0.5, 0.5),
        "w_atom_out": normal_values(splits[3], (CA, CA), CA ** -0.5, 0.5),
        "w_atom_up": normal_values(splits[4], (CA, D), CA ** -0.5, 0.5),
        "pair_repr": normal_values(splits[5], (NTOK, N_ROW, TOK_ROW, CP), 1.0, 6.0, ((0, 8), (2, 16))),
        "w_bias": draw_w_bias(jax.random.fold_in(splits[12], 71), 0),
        "w_query": normal_values(splits[7], (D, D), D ** -0.5, 0.21875),
        "w_kv": normal_values(splits[8], (D, 2 * D), D ** -0.5, 0.21875),
        "w_gate": normal_values(splits[9], (D, D), D ** -0.5, 0.21875),
        "w_out": normal_values(splits[10], (D, D), D ** -0.5, 0.21875),
        "w_down": normal_values(splits[11], (D, CA), D ** -0.5, 0.21875),
    }


EPS = 1e-05

def layer_norm(values):
    center = lax.optimization_barrier(jnp.mean(values, axis=-1, keepdims=True))
    spread = lax.optimization_barrier(jnp.mean(values * values, axis=-1, keepdims=True)) - center * center
    return (values - center) / jnp.sqrt(spread + EPS)

def atom_layer(atom_feat, w_atom_qkv, w_atom_out):
    total = atom_feat.shape[0]
    atom_proj = jnp.dot(atom_feat, w_atom_qkv, preferred_element_type=jnp.float32).astype(jnp.bfloat16)
    queries = atom_proj[:, :CA]
    keyvals = jnp.pad(atom_proj[:, CA:], ((HALO, HALO), (0, 0)))
    blocks = total // QBLOCK
    window = (jnp.arange(blocks)[:, None] * QBLOCK + jnp.arange(KWIN)[None, :]).astype(jnp.int32)
    position = window - HALO
    valid = (position >= 0) & (position < total)
    near = keyvals[window]
    near_keys = near[..., :CA].reshape(blocks, KWIN, AHEADS, ADH).astype(jnp.float32)
    near_vals = near[..., CA:].reshape(blocks, KWIN, AHEADS, ADH).astype(jnp.float32)
    block_q = queries.reshape(blocks, QBLOCK, AHEADS, ADH).astype(jnp.float32)
    scores = jnp.einsum('bqhd,bkhd->bhqk', block_q, near_keys) / ADH ** 0.5
    scores = jnp.where(valid[:, None, None, :], scores, -1e+30)
    top = lax.optimization_barrier(jnp.max(scores, axis=-1, keepdims=True))
    expo = jnp.exp(scores - top)
    atom_weights = expo.astype(jnp.bfloat16)
    denom = lax.optimization_barrier(jnp.sum(expo, axis=-1))
    context = jnp.einsum('bhqk,bkhd->bqhd', atom_weights.astype(jnp.float32), near_vals)
    context = context / jnp.transpose(denom, (0, 2, 1))[..., None]
    atom_ctx = context.reshape(total, CA).astype(jnp.bfloat16)
    mixed = atom_feat.astype(jnp.float32) + jnp.dot(atom_ctx, w_atom_out, preferred_element_type=jnp.float32)
    return mixed.astype(jnp.bfloat16)

def reference(atom_feat, atom_token, w_atom_qkv, w_atom_out, w_atom_up, pair_repr, w_bias, w_query, w_kv, w_gate, w_out, w_down):
    atom_out = atom_layer(atom_feat, w_atom_qkv, w_atom_out)
    atom_up = jax.nn.relu(jnp.dot(atom_out, w_atom_up, preferred_element_type=jnp.float32)).astype(jnp.bfloat16)
    token_sum = jax.ops.segment_sum(atom_up.astype(jnp.float32), atom_token, num_segments=NTOK)
    counts = jax.ops.segment_sum(jnp.ones(atom_token.shape, jnp.float32), atom_token, num_segments=NTOK)
    token_act = token_sum / counts[:, None]
    normed = layer_norm(token_act).astype(jnp.bfloat16)
    queries = jnp.dot(normed, w_query, preferred_element_type=jnp.float32).astype(jnp.bfloat16)
    keyvals = jnp.dot(normed, w_kv, preferred_element_type=jnp.float32).astype(jnp.bfloat16)
    gating = jax.nn.sigmoid(jnp.dot(normed, w_gate, preferred_element_type=jnp.float32))
    all_keys = keyvals[:, :D].reshape(NTOK, HEADS, DH).astype(jnp.float32)
    all_vals = keyvals[:, D:].reshape(NTOK, HEADS, DH).astype(jnp.float32)
    tiles = pair_repr.reshape(N_ROW, TOK_ROW, NTOK, CP)

    def one_block(inputs):
        tile, block_q, block_gate, block_act = inputs
        pair_normed = layer_norm(tile.astype(jnp.float32)).astype(jnp.bfloat16)
        pair_bias = jnp.dot(pair_normed.reshape(-1, CP), w_bias.astype(jnp.bfloat16), preferred_element_type=jnp.float32).astype(jnp.bfloat16)
        pair_bias = pair_bias.reshape(TOK_ROW, NTOK, HEADS)
        query_heads = block_q.reshape(TOK_ROW, HEADS, DH).astype(jnp.float32)
        scores = jnp.einsum('qhd,khd->hqk', query_heads, all_keys) / DH ** 0.5
        scores = scores + jnp.transpose(pair_bias, (2, 0, 1)).astype(jnp.float32)
        top = lax.optimization_barrier(jnp.max(scores, axis=-1, keepdims=True))
        expo = jnp.exp(scores - top)
        token_weights = expo.astype(jnp.bfloat16)
        denom = lax.optimization_barrier(jnp.sum(expo, axis=-1))
        context = jnp.einsum('hqk,khd->qhd', token_weights.astype(jnp.float32), all_vals)
        context = context / jnp.transpose(denom)[:, :, None]
        gated = (context.reshape(TOK_ROW, D) * block_gate).astype(jnp.bfloat16)
        updated = block_act + jnp.dot(gated, w_out, preferred_element_type=jnp.float32)
        return updated.astype(jnp.bfloat16)
    token_out = lax.map(one_block, (tiles, queries.reshape(N_ROW, TOK_ROW, D), gating.reshape(N_ROW, TOK_ROW, D), token_act.reshape(N_ROW, TOK_ROW, D)))
    token_out = token_out.reshape(NTOK, D)
    token_down = jnp.dot(token_out, w_down, preferred_element_type=jnp.float32).astype(jnp.bfloat16)
    atom_final = atom_out.astype(jnp.float32) + token_down[atom_token].astype(jnp.float32)
    return (token_out, atom_final.astype(jnp.bfloat16))
```

```python
import functools

import jax
import jax.numpy as jnp
from jax import lax
from jax.experimental import pallas as pl
from jax.experimental.pallas import tpu as pltpu
from jax.sharding import PartitionSpec as P

MESH = pl.DeviceIdType.MESH
F32 = jnp.float32
BF16 = jnp.bfloat16

EPS = 1e-05
AHEADS = 4
QBLOCK = 32
KWIN = 128
HALO = 48
EXT = 256
CHUNK = 16
PIECES = 4
LANES = 128
VOFF = 64
WINDOW = 256


def dot(a, b, dims=((1,), (0,))):
    return lax.dot_general(a, b, (dims, ((), ())), preferred_element_type=F32)


def iota(shape, dim):
    return lax.broadcasted_iota(jnp.int32, shape, dim)


def kernel(
    feat, tok, w_qkv, w_ao, w_up, pair, w_bias, w_query, w_kv, w_gate, w_out, w_down,
    out_tok, out_atom,
    xbuf, v_qkv, v_ao, v_up, v_bias, v_q, v_k, v_v, v_g, v_o, v_d,
    ext, tok_all, atoms_all, onehot, stage, bias_out, bias_in,
    wsel, w_out_t, act_t, kv_own, kv_all, g_all,
    load_sem, pair_sem, halo_send, halo_recv, tok_send, tok_recv,
    atom_send, atom_recv, bias_send, bias_recv, kv_send, kv_recv, g_send, g_recv,
):
    rows, cols = lax.axis_size("row"), lax.axis_size("col")
    r, c = lax.axis_index("row"), lax.axis_index("col")
    flat = r * cols + c
    devices = rows * cols
    atoms, chans = feat.shape
    tokens, _, share, _ = pair.shape
    keys = rows * share
    width = w_query.shape[0]
    head = width // cols

    loads = []

    def load(src, dst, sem=None):
        copy = pltpu.make_async_copy(src, dst, load_sem.at[len(loads)] if sem is None else sem)
        copy.start()
        if sem is None:
            loads.append(copy)
        return copy

    load_feat = load(feat, ext.at[pl.ds(HALO, atoms)])
    load_tok = load(tok, tok_all.at[c])
    load_bias = load(w_bias, v_bias)
    part = tokens // PIECES
    load_pair = [load(pair.at[pl.ds(0, part)], xbuf.at[pl.ds(0, part)], pair_sem.at[0])]
    load_qkv = load(w_qkv, v_qkv)
    load_ao = load(w_ao, v_ao)
    for i in range(1, PIECES):
        load_pair.append(
            load(pair.at[pl.ds(i * part, part)], xbuf.at[pl.ds(i * part, part)], pair_sem.at[i])
        )
    load_up = load(w_up, v_up)
    first = jnp.minimum(c * head // LANES, (width - WINDOW) // LANES)
    begin = pl.multiple_of(first * LANES, LANES)
    window = pl.ds(begin, WINDOW)
    load_q = load(w_query.at[:, window], v_q)
    load_g = load(w_gate.at[:, window], v_g)
    load_k = load(w_kv.at[:, window], v_k)
    load_v = load(w_kv.at[:, pl.ds(pl.multiple_of(width + begin, LANES), WINDOW)], v_v)
    load_o = load(w_out, v_o)
    load_d = load(w_down, v_d)

    barrier = pltpu.get_barrier_semaphore()
    right, left = lax.rem(flat + 1, devices), lax.rem(flat + devices - 1, devices)

    def coords(index):
        return (index // cols, lax.rem(index, cols))

    for peer in (left, right):
        pl.semaphore_signal(barrier, inc=1, device_id=coords(peer), device_id_type=MESH)
    for d in range(1, cols):
        pl.semaphore_signal(
            barrier, inc=1, device_id=(r, lax.rem(c + d, cols)), device_id_type=MESH
        )
    for d in range(1, rows):
        pl.semaphore_signal(
            barrier, inc=1, device_id=(lax.rem(r + d, rows), c), device_id_type=MESH
        )
    ext[pl.ds(atoms + 2 * HALO, EXT - atoms - 2 * HALO), :] = jnp.zeros(
        (EXT - atoms - 2 * HALO, chans), BF16
    )
    pl.semaphore_wait(barrier, cols + rows)

    to_right = pltpu.make_async_remote_copy(
        src_ref=feat.at[pl.ds(atoms - HALO, HALO)],
        dst_ref=ext.at[pl.ds(0, HALO)],
        send_sem=halo_send.at[0],
        recv_sem=halo_recv.at[0],
        device_id=coords(right),
        device_id_type=MESH,
    )
    to_left = pltpu.make_async_remote_copy(
        src_ref=feat.at[pl.ds(0, HALO)],
        dst_ref=ext.at[pl.ds(HALO + atoms, HALO)],
        send_sem=halo_send.at[1],
        recv_sem=halo_recv.at[1],
        device_id=coords(left),
        device_id_type=MESH,
    )
    to_right.start()
    to_left.start()

    def col_copy(src, dst, send, recv, d):
        return pltpu.make_async_remote_copy(
            src_ref=src,
            dst_ref=dst,
            send_sem=send.at[d],
            recv_sem=recv.at[d],
            device_id=(r, lax.rem(c + d, cols)),
            device_id_type=MESH,
        )

    load_tok.wait()
    tok_copies = [
        col_copy(tok_all.at[c], tok_all.at[c], tok_send, tok_recv, d) for d in range(1, cols)
    ]
    for copy in tok_copies:
        copy.start()

    load_bias.wait()
    eye = (iota((LANES, LANES), 0) == iota((LANES, LANES), 1)).astype(BF16)
    wb_t = dot(v_bias[...].astype(BF16), eye, ((0,), (0,))).astype(BF16)
    wb_sum = jnp.sum(wb_t.astype(F32), axis=1, keepdims=True)
    heads = wb_t.shape[0]
    lhs = jnp.concatenate([wb_t, jnp.ones((16, LANES), BF16)], axis=0)
    ones = jnp.ones((16, LANES), BF16)

    def pair_chunk(index):
        start = pl.multiple_of(index * CHUNK, CHUNK)
        x = xbuf[pl.ds(start, CHUNK)].reshape(CHUNK * keys, LANES)
        x32 = x.astype(F32)
        square = x32 * x32
        high = square.astype(BF16)
        low = (square - high.astype(F32)).astype(BF16)
        proj = dot(lhs, x, ((1,), (1,)))
        squares = dot(ones, high, ((1,), (1,))) + dot(ones, low, ((1,), (1,)))
        mean = proj[heads:heads + 8] * (1.0 / LANES)
        var = squares[:8] * (1.0 / LANES) - mean * mean
        scale = lax.rsqrt(var + EPS)
        mean = jnp.concatenate([mean] * (heads // 8), axis=0)
        scale = jnp.concatenate([scale] * (heads // 8), axis=0)
        bias = (proj[:heads] - mean * wb_sum) * scale
        for q in range(CHUNK):
            stage[pl.ds(q, heads, stride=CHUNK), :] = bias[:, q * keys:(q + 1) * keys]
        for h in range(heads):
            bias_out[h, pl.ds(start, CHUNK), :] = stage[pl.ds(h * CHUNK, CHUNK), :].astype(BF16)

    def bias_copy(i, d):
        span = pl.ds(i * part, part)
        return col_copy(
            bias_out.at[lax.rem(c + d, cols), span], bias_in.at[c, span], bias_send, bias_recv, d
        )

    def pair_piece(i):
        load_pair[i].wait()
        steps = part // CHUNK

        def step(k, carry):
            pair_chunk(i * steps + k)
            return carry

        lax.fori_loop(0, steps, step, 0)

    def send_piece(i):
        for d in range(1, cols):
            bias_copy(i, d).start()

    pair_piece(0)

    load_feat.wait()
    load_qkv.wait()
    load_ao.wait()
    to_right.wait()
    to_left.wait()
    proj = dot(ext[...], v_qkv[...]).astype(BF16)
    queries = proj[HALO:HALO + atoms, :chans]
    near_keys = proj[:, chans:2 * chans]
    near_vals = proj[:, 2 * chans:]
    lane_head = iota((atoms, chans), 1) // (chans // AHEADS)
    by_head = jnp.concatenate(
        [jnp.where(lane_head == h, queries, jnp.zeros_like(queries)) for h in range(AHEADS)], axis=0
    )
    scores = dot(by_head, near_keys, ((1,), (1,))) * (chans // AHEADS) ** -0.5
    block = lax.rem(iota(scores.shape, 0), atoms) // QBLOCK * QBLOCK
    offset = iota(scores.shape, 1)
    position = flat * atoms + offset - HALO
    valid = (offset >= block) & (offset < block + KWIN)
    valid = valid & (position >= 0) & (position < devices * atoms)
    scores = jnp.where(valid, scores, -1e30)
    expo = jnp.exp(scores - jnp.max(scores, axis=1, keepdims=True))
    denom = jnp.sum(expo, axis=1, keepdims=True)
    mixed = dot(expo.astype(BF16), near_vals) / denom
    context = jnp.zeros((atoms, chans), F32)
    for h in range(AHEADS):
        context = jnp.where(lane_head == h, mixed[h * atoms:(h + 1) * atoms], context)
    atom_out = ext[pl.ds(HALO, atoms), :].astype(F32) + dot(context.astype(BF16), v_ao[...])
    atoms_all[c] = atom_out.astype(BF16)
    atom_copies = [
        col_copy(atoms_all.at[c], atoms_all.at[c], atom_send, atom_recv, d) for d in range(1, cols)
    ]
    for copy in atom_copies:
        copy.start()

    send_piece(0)
    for i in range(1, PIECES):
        pair_piece(i)
        send_piece(i)

    load_q.wait()
    load_g.wait()
    load_k.wait()
    load_v.wait()
    source = iota((WINDOW, LANES), 0) - (c * head - begin)
    target = iota((WINDOW, LANES), 1)
    pick_low = ((source == target) & (target < head)).astype(BF16)
    pick_high = ((source == target - VOFF) & (target >= VOFF) & (target < VOFF + head)).astype(BF16)
    wsel[:, 0:LANES] = dot(v_q[...], pick_low).astype(BF16)
    wsel[:, LANES:2 * LANES] = dot(v_g[...], pick_high).astype(BF16)
    wsel[:, 2 * LANES:] = (dot(v_k[...], pick_low) + dot(v_v[...], pick_high)).astype(BF16)

    for copy in tok_copies:
        copy.wait()
    count = jnp.zeros((tokens, atoms), F32)
    token_of = iota((tokens, atoms), 0) + r * tokens
    for j in range(cols):
        hit = (tok_all[j] == token_of).astype(F32)
        count = count + hit
        onehot[j] = hit.astype(BF16)
    count = 1.0 / jnp.sum(count, axis=1, keepdims=True)

    load_up.wait()
    for copy in atom_copies:
        copy.wait()
    total = jnp.zeros((tokens, width), F32)
    group = 4
    for j in range(0, cols, group):
        cells = atoms_all[pl.ds(j, group)].reshape(group * atoms, chans)
        up = jnp.maximum(dot(cells, v_up[...]), 0.0).astype(BF16)
        hits = jnp.concatenate([onehot[j + k] for k in range(group)], axis=1)
        total = total + dot(hits, up)
    act = total * count
    center = jnp.mean(act, axis=1, keepdims=True)
    spread = jnp.mean(act * act, axis=1, keepdims=True) - center * center
    normed = ((act - center) * lax.rsqrt(spread + EPS)).astype(BF16)
    projected = dot(normed, wsel[...])
    kv_own[...] = projected[:, 2 * LANES:].astype(BF16).reshape(kv_own.shape)
    kv_copies = [
        pltpu.make_async_remote_copy(
            src_ref=kv_own,
            dst_ref=kv_all.at[:, r],
            send_sem=kv_send.at[d],
            recv_sem=kv_recv.at[d],
            device_id=(lax.rem(r + d, rows), c),
            device_id_type=MESH,
        )
        for d in range(1, rows)
    ]
    for copy in kv_copies:
        copy.start()
    kv_all[:, r] = kv_own[...]
    head_q = projected[:, :LANES].astype(BF16)
    gate = jax.nn.sigmoid(projected[:, LANES:2 * LANES])
    act_t[...] = act.T
    load_o.wait()
    w_out_t[...] = v_o[...].T
    bias_in[c] = bias_out[c]

    for copy in kv_copies:
        copy.wait()
    for d in range(1, cols):
        col_copy(
            bias_out.at[lax.rem(c + d, cols)], bias_in.at[c], bias_send, bias_recv, d
        ).wait()
    key_vals = kv_all[...].reshape(cols * keys, LANES)
    scores = dot(head_q, key_vals, ((1,), (1,))) * head ** -0.5
    scores = scores + jnp.concatenate([bias_in[j].astype(F32) for j in range(cols)], axis=1)
    expo = jnp.exp(scores - jnp.max(scores, axis=1, keepdims=True))
    denom = jnp.sum(expo, axis=1, keepdims=True)
    gated = dot(expo.astype(BF16), key_vals) / denom * gate
    g_all[c] = gated.T[VOFF:VOFF + head].astype(BF16)
    g_copies = [col_copy(g_all.at[c], g_all.at[c], g_send, g_recv, d) for d in range(1, cols)]
    for copy in g_copies:
        copy.start()
    load_d.wait()
    w_down_t = v_d[...].T
    own_hits = onehot[c].astype(F32).T.astype(BF16)

    for copy in g_copies:
        copy.wait()
    mixed = dot(w_out_t[...], g_all[...].reshape(width, tokens))
    token_out = (act_t[...] + mixed).astype(BF16)
    token_down = dot(w_down_t, token_out).astype(BF16)
    final = atoms_all[c].astype(F32) + dot(own_hits, token_down, ((1,), (1,)))
    out_atom[...] = final.astype(BF16)
    w_out_t[:, 0:tokens] = token_out
    own = w_out_t[pl.ds(pl.multiple_of(c * head, head), head), 0:tokens]
    out_tok[...] = own.astype(F32).T.astype(BF16)


def body(
    atom_feat, atom_token, w_atom_qkv, w_atom_out, w_atom_up, pair_repr, w_bias, w_query, w_kv,
    w_gate, w_out, w_down,
):
    rows, cols = lax.axis_size("row"), lax.axis_size("col")
    atoms, chans = atom_feat.shape
    tokens, _, share, pair_width = pair_repr.shape
    keys = rows * share
    width = w_query.shape[0]
    head = width // cols
    heads = w_bias.shape[1]
    vmem = pltpu.VMEM
    sems = lambda n: pltpu.SemaphoreType.DMA((n,))
    return pl.pallas_call(
        kernel,
        out_shape=(
            jax.ShapeDtypeStruct((tokens, head), BF16),
            jax.ShapeDtypeStruct((atoms, chans), BF16),
        ),
        in_specs=[pl.BlockSpec(memory_space=pl.ANY)] * 12,
        out_specs=[pl.BlockSpec(memory_space=pltpu.VMEM)] * 2,
        scratch_shapes=[
            vmem(pair_repr.shape, BF16),
            vmem(w_atom_qkv.shape, BF16),
            vmem(w_atom_out.shape, BF16),
            vmem(w_atom_up.shape, BF16),
            vmem(w_bias.shape, F32),
            vmem((width, WINDOW), BF16),
            vmem((width, WINDOW), BF16),
            vmem((width, WINDOW), BF16),
            vmem((width, WINDOW), BF16),
            vmem(w_out.shape, BF16),
            vmem(w_down.shape, BF16),
            vmem((EXT, chans), BF16),
            vmem((cols, 1, atoms), jnp.int32),
            vmem((cols, atoms, chans), BF16),
            vmem((cols, tokens, atoms), BF16),
            vmem((heads * CHUNK, keys), F32),
            vmem((heads, tokens, keys), BF16),
            vmem((cols, tokens, keys), BF16),
            vmem((width, 3 * LANES), BF16),
            vmem(w_out.shape, BF16),
            vmem((width, tokens), F32),
            vmem((cols, share, LANES), BF16),
            vmem((cols, rows, share, LANES), BF16),
            vmem((cols, head, tokens), BF16),
            sems(13),
            sems(PIECES),
            sems(2),
            sems(2),
            sems(cols),
            sems(cols),
            sems(cols),
            sems(cols),
            sems(cols),
            sems(cols),
            sems(rows),
            sems(rows),
            sems(cols),
            sems(cols),
        ],
        compiler_params=pltpu.CompilerParams(
            collective_id=0, has_side_effects=True, vmem_limit_bytes=56 * 1024 * 1024
        ),
    )(
        atom_feat, atom_token.reshape(1, atoms), w_atom_qkv, w_atom_out, w_atom_up, pair_repr,
        w_bias, w_query, w_kv, w_gate, w_out, w_down,
    )


def solution(mesh):
    return jax.shard_map(
        body,
        mesh=mesh,
        in_specs=(
            P(("row", "col"), None),
            P(("row", "col")),
            P(),
            P(),
            P(),
            P("row", None, "col", None),
            P(),
            P(),
            P(),
            P(),
            P(),
            P(),
        ),
        out_specs=(P("row", "col"), P(("row", "col"), None)),
        check_vma=False,
    )
```

```python
import functools

import jax
import jax.numpy as jnp
from jax import lax
from jax.experimental import pallas as pl
from jax.experimental.pallas import tpu as pltpu
from jax.sharding import PartitionSpec as P

MESH = pl.DeviceIdType.MESH
F32 = jnp.float32
BF16 = jnp.bfloat16

EPS = 1e-05
AHEADS = 4
QBLOCK = 32
KWIN = 128
HALO = 48
EXT = 256
CHUNK = 16
PIECES = 8
AHEAD = 2
BEFORE = 1
EARLY = 3
EARLY_SENT = 3
LANES = 128
VOFF = 64
ORDER = (5, 10, 15, 4, 1, 11, 14, 7, 8, 2, 13, 6, 9, 3, 12)
WINDOW = 256


def dot(a, b, dims=((1,), (0,))):
    return lax.dot_general(a, b, (dims, ((), ())), preferred_element_type=F32)


def iota(shape, dim):
    return lax.broadcasted_iota(jnp.int32, shape, dim)


def kernel(
    feat, tok, w_qkv, w_ao, w_up, pair, w_bias, w_query, w_kv, w_gate, w_out, w_down,
    out_tok, out_atom,
    xbuf, v_qkv, v_ao, v_up, v_bias, v_q, v_k, v_v, v_g, v_o, v_d,
    ext, tok_all, atoms_all, own_hits, total, count, stage, bias_out, bias_in,
    wsel, w_out_t, act_t, kv_own, kv_all, g_all,
    load_sem, pair_sem, halo_send, halo_recv, tok_send, tok_recv,
    atom_send, atom_recv, bias_send, bias_recv, kv_send, kv_recv, g_send, g_recv,
):
    rows, cols = lax.axis_size("row"), lax.axis_size("col")
    r, c = lax.axis_index("row"), lax.axis_index("col")
    flat = r * cols + c
    devices = rows * cols
    atoms, chans = feat.shape
    tokens, _, share, _ = pair.shape
    keys = rows * share
    width = w_query.shape[0]
    head = width // cols

    names = ("feat", "tok", "bias", "qkv", "ao", "up", "q", "g", "k", "v", "o", "d")
    part = tokens // PIECES
    first = jnp.minimum(c * head // LANES, (width - WINDOW) // LANES)
    begin = pl.multiple_of(first * LANES, LANES)
    window = pl.ds(begin, WINDOW)
    beside = pl.ds(pl.multiple_of(width + begin, LANES), WINDOW)
    ends = {
        "feat": (feat, ext.at[pl.ds(HALO, atoms)]),
        "tok": (tok, tok_all.at[c]),
        "bias": (w_bias, v_bias),
        "qkv": (w_qkv, v_qkv),
        "ao": (w_ao, v_ao),
        "up": (w_up, v_up),
        "q": (w_query.at[:, window], v_q),
        "g": (w_gate.at[:, window], v_g),
        "k": (w_kv.at[:, window], v_k),
        "v": (w_kv.at[:, beside], v_v),
        "o": (w_out, v_o),
        "d": (w_down, v_d),
    }
    loads = {
        name: pltpu.make_async_copy(*ends[name], load_sem.at[i]) for i, name in enumerate(names)
    }
    pair_loads = [
        pltpu.make_async_copy(
            pair.at[pl.ds(i * part, part)], xbuf.at[pl.ds(i * part, part)], pair_sem.at[i]
        )
        for i in range(PIECES)
    ]
    for name in ("feat", "tok", "bias"):
        loads[name].start()
    for i in range(AHEAD):
        pair_loads[i].start()
    for name in ("qkv", "ao"):
        loads[name].start()

    def col_copy(src, dst, send, recv, d):
        return pltpu.make_async_remote_copy(
            src_ref=src,
            dst_ref=dst,
            send_sem=send.at[d],
            recv_sem=recv.at[d],
            device_id=(r, lax.rem(c + d, cols)),
            device_id_type=MESH,
        )

    barrier = pltpu.get_barrier_semaphore()
    right, left = lax.rem(flat + 1, devices), lax.rem(flat + devices - 1, devices)

    def coords(index):
        return (index // cols, lax.rem(index, cols))

    for peer in (left, right):
        pl.semaphore_signal(barrier, inc=1, device_id=coords(peer), device_id_type=MESH)
    for d in range(1, cols):
        pl.semaphore_signal(
            barrier, inc=1, device_id=(r, lax.rem(c + d, cols)), device_id_type=MESH
        )
    for d in range(1, rows):
        pl.semaphore_signal(
            barrier, inc=1, device_id=(lax.rem(r + d, rows), c), device_id_type=MESH
        )
    ext[pl.ds(atoms + 2 * HALO, EXT - atoms - 2 * HALO), :] = jnp.zeros(
        (EXT - atoms - 2 * HALO, chans), BF16
    )

    loads["bias"].wait()
    wb_t = v_bias[...].astype(BF16)
    wb_sum = jnp.sum(wb_t.astype(F32), axis=1, keepdims=True)
    heads = wb_t.shape[0]
    lhs = jnp.concatenate([wb_t, jnp.ones((16, LANES), BF16)], axis=0)
    ones = jnp.ones((16, LANES), BF16)

    def pair_chunk(index):
        start = pl.multiple_of(index * CHUNK, CHUNK)
        x = xbuf[pl.ds(start, CHUNK)].reshape(CHUNK * keys, LANES)
        x32 = x.astype(F32)
        square = x32 * x32
        high = square.astype(BF16)
        low = (square - high.astype(F32)).astype(BF16)
        proj = dot(lhs, x, ((1,), (1,)))
        squares = dot(ones, high, ((1,), (1,))) + dot(ones, low, ((1,), (1,)))
        mean = proj[heads:heads + 8] * (1.0 / LANES)
        var = squares[:8] * (1.0 / LANES) - mean * mean
        scale = lax.rsqrt(var + EPS)
        mean = jnp.concatenate([mean] * (heads // 8), axis=0)
        scale = jnp.concatenate([scale] * (heads // 8), axis=0)
        bias = (proj[:heads] - mean * wb_sum) * scale
        for q in range(CHUNK):
            stage[pl.ds(q, heads, stride=CHUNK), :] = bias[:, q * keys:(q + 1) * keys]
        for h in range(heads):
            bias_out[h, pl.ds(start, CHUNK), :] = stage[pl.ds(h * CHUNK, CHUNK), :].astype(BF16)

    def bias_copy(i, d):
        span = pl.ds(i * part, part)
        return col_copy(
            bias_out.at[lax.rem(c + d, cols), span], bias_in.at[c, span], bias_send, bias_recv, d
        )

    def pair_piece(i):
        pair_loads[i].wait()
        if i + AHEAD < PIECES:
            pair_loads[i + AHEAD].start()
        steps = part // CHUNK

        def step(k, carry):
            pair_chunk(i * steps + k)
            return carry

        lax.fori_loop(0, steps, step, 0)

    def send_piece(i):
        for d in ORDER:
            bias_copy(i, d).start()

    for i in range(BEFORE):
        pair_piece(i)
    pl.semaphore_wait(barrier, cols + rows)

    to_right = pltpu.make_async_remote_copy(
        src_ref=feat.at[pl.ds(atoms - HALO, HALO)],
        dst_ref=ext.at[pl.ds(0, HALO)],
        send_sem=halo_send.at[0],
        recv_sem=halo_recv.at[0],
        device_id=coords(right),
        device_id_type=MESH,
    )
    to_left = pltpu.make_async_remote_copy(
        src_ref=feat.at[pl.ds(0, HALO)],
        dst_ref=ext.at[pl.ds(HALO + atoms, HALO)],
        send_sem=halo_send.at[1],
        recv_sem=halo_recv.at[1],
        device_id=coords(left),
        device_id_type=MESH,
    )
    to_right.start()
    to_left.start()

    loads["tok"].wait()
    tok_copies = [
        col_copy(tok_all.at[c], tok_all.at[c], tok_send, tok_recv, d) for d in range(1, cols)
    ]
    for copy in tok_copies:
        copy.start()
    for i in range(min(BEFORE, EARLY_SENT)):
        send_piece(i)

    for i in range(BEFORE, EARLY):
        pair_piece(i)
        if i < EARLY_SENT:
            send_piece(i)

    loads["feat"].wait()
    loads["qkv"].wait()
    loads["ao"].wait()
    to_right.wait()
    to_left.wait()
    proj = dot(ext[...], v_qkv[...]).astype(BF16)
    queries = proj[HALO:HALO + atoms, :chans]
    near_keys = proj[:, chans:2 * chans]
    near_vals = proj[:, 2 * chans:]
    lane_head = iota((atoms, chans), 1) // (chans // AHEADS)
    by_head = jnp.concatenate(
        [jnp.where(lane_head == h, queries, jnp.zeros_like(queries)) for h in range(AHEADS)], axis=0
    )
    scores = dot(by_head, near_keys, ((1,), (1,))) * (chans // AHEADS) ** -0.5
    block = lax.rem(iota(scores.shape, 0), atoms) // QBLOCK * QBLOCK
    offset = iota(scores.shape, 1)
    position = flat * atoms + offset - HALO
    valid = (offset >= block) & (offset < block + KWIN)
    valid = valid & (position >= 0) & (position < devices * atoms)
    scores = jnp.where(valid, scores, -1e30)
    expo = jnp.exp(scores - jnp.max(scores, axis=1, keepdims=True))
    denom = jnp.sum(expo, axis=1, keepdims=True)
    mixed = dot(expo.astype(BF16), near_vals) / denom
    context = jnp.zeros((atoms, chans), F32)
    for h in range(AHEADS):
        context = jnp.where(lane_head == h, mixed[h * atoms:(h + 1) * atoms], context)
    atom_out = ext[pl.ds(HALO, atoms), :].astype(F32) + dot(context.astype(BF16), v_ao[...])
    atoms_all[c] = atom_out.astype(BF16)
    atom_copies = [
        col_copy(atoms_all.at[c], atoms_all.at[c], atom_send, atom_recv, d) for d in ORDER
    ]
    for copy in atom_copies:
        copy.start()

    for name in ("up", "q", "g", "k", "v"):
        loads[name].start()
    for i in range(EARLY_SENT, EARLY):
        send_piece(i)
    for copy in tok_copies:
        copy.wait()

    token_of = iota((tokens, atoms), 0) + r * tokens
    arrival = (0,) + ORDER
    group = 4

    def token_group(j):
        cells, hits = [], []
        for d in arrival[j * group:(j + 1) * group]:
            if d:
                atom_copies[ORDER.index(d)].wait()
            slot = lax.rem(c + cols - d, cols)
            cells.append(atoms_all[slot])
            hits.append((tok_all[slot] == token_of).astype(F32))
        if j == 0:
            loads["up"].wait()
            own_hits[...] = hits[0].T.astype(BF16)
        up = jnp.maximum(dot(jnp.concatenate(cells, axis=0), v_up[...]), 0.0).astype(BF16)
        added = dot(jnp.concatenate(hits, axis=1).astype(BF16), up)
        counted = sum(hits[1:], hits[0])
        total[...] = added if j == 0 else total[...] + added
        count[...] = counted if j == 0 else count[...] + counted

    for i in range(EARLY, PIECES):
        pair_piece(i)
        send_piece(i)
        if i == PIECES - 3:
            loads["q"].wait()
            loads["g"].wait()
            loads["k"].wait()
            loads["v"].wait()
            source = iota((WINDOW, LANES), 0) - (c * head - begin)
            target = iota((WINDOW, LANES), 1)
            pick_low = ((source == target) & (target < head)).astype(BF16)
            pick_high = ((source == target - VOFF) & (target >= VOFF) & (target < VOFF + head)).astype(BF16)
            wsel[:, 0:LANES] = dot(v_q[...], pick_low).astype(BF16)
            wsel[:, LANES:2 * LANES] = dot(v_g[...], pick_high).astype(BF16)
            wsel[:, 2 * LANES:] = (dot(v_k[...], pick_low) + dot(v_v[...], pick_high)).astype(BF16)
        if i >= PIECES - 2:
            token_group(i - PIECES + 2)
    for name in ("o", "d"):
        loads[name].start()
    for j in range(2, cols // group):
        token_group(j)
    act = total[...] * (1.0 / jnp.sum(count[...], axis=1, keepdims=True))
    center = jnp.mean(act, axis=1, keepdims=True)
    spread = jnp.mean(act * act, axis=1, keepdims=True) - center * center
    normed = ((act - center) * lax.rsqrt(spread + EPS)).astype(BF16)
    projected = dot(normed, wsel[...])
    kv_own[...] = projected[:, 2 * LANES:].astype(BF16).reshape(kv_own.shape)
    kv_copies = [
        pltpu.make_async_remote_copy(
            src_ref=kv_own,
            dst_ref=kv_all.at[:, r],
            send_sem=kv_send.at[d],
            recv_sem=kv_recv.at[d],
            device_id=(lax.rem(r + d, rows), c),
            device_id_type=MESH,
        )
        for d in range(1, rows)
    ]
    for copy in kv_copies:
        copy.start()
    kv_all[:, r] = kv_own[...]
    head_q = projected[:, :LANES].astype(BF16)
    gate = jax.nn.sigmoid(projected[:, LANES:2 * LANES])
    act_t[...] = act.T
    loads["o"].wait()
    w_out_t[...] = v_o[...].T
    bias_in[c] = bias_out[c]

    for copy in kv_copies:
        copy.wait()
    for d in range(1, cols):
        col_copy(
            bias_out.at[lax.rem(c + d, cols)], bias_in.at[c], bias_send, bias_recv, d
        ).wait()
    key_vals = kv_all[...].reshape(cols * keys, LANES)
    scores = dot(head_q, key_vals, ((1,), (1,))) * head ** -0.5
    scores = scores + jnp.concatenate([bias_in[j].astype(F32) for j in range(cols)], axis=1)
    expo = jnp.exp(scores - jnp.max(scores, axis=1, keepdims=True))
    denom = jnp.sum(expo, axis=1, keepdims=True)
    gated = dot(expo.astype(BF16), key_vals) / denom * gate
    g_all[c] = gated.T[VOFF:VOFF + head].astype(BF16)
    g_copies = [col_copy(g_all.at[c], g_all.at[c], g_send, g_recv, d) for d in ORDER]
    for copy in g_copies:
        copy.start()
    loads["d"].wait()
    w_down_t = v_d[...].T

    for copy in g_copies:
        copy.wait()
    mixed = dot(w_out_t[...], g_all[...].reshape(width, tokens))
    token_out = (act_t[...] + mixed).astype(BF16)
    token_down = dot(w_down_t, token_out).astype(BF16)
    final = atoms_all[c].astype(F32) + dot(own_hits[...], token_down, ((1,), (1,)))
    out_atom[...] = final.astype(BF16)
    w_out_t[:, 0:tokens] = token_out
    out_tok[...] = w_out_t[pl.ds(pl.multiple_of(c * head, head), head), 0:tokens]


def hand_out(token_in, atom_in, token_out, atom_out):
    token_out[...] = token_in[...]
    atom_out[...] = atom_in[...]


def body(
    atom_feat, atom_token, w_atom_qkv, w_atom_out, w_atom_up, pair_repr, w_bias, w_query, w_kv,
    w_gate, w_out, w_down,
):
    rows, cols = lax.axis_size("row"), lax.axis_size("col")
    atoms, chans = atom_feat.shape
    tokens, _, share, pair_width = pair_repr.shape
    keys = rows * share
    width = w_query.shape[0]
    head = width // cols
    heads = w_bias.shape[1]
    vmem = pltpu.VMEM
    sems = lambda n: pltpu.SemaphoreType.DMA((n,))
    token_out, atom_final = pl.pallas_call(
        kernel,
        out_shape=(
            jax.ShapeDtypeStruct((head, tokens), BF16),
            jax.ShapeDtypeStruct((atoms, chans), BF16),
        ),
        in_specs=[pl.BlockSpec(memory_space=pl.ANY)] * 12,
        out_specs=[pl.BlockSpec(memory_space=pltpu.VMEM)] * 2,
        scratch_shapes=[
            vmem(pair_repr.shape, BF16),
            vmem(w_atom_qkv.shape, BF16),
            vmem(w_atom_out.shape, BF16),
            vmem(w_atom_up.shape, BF16),
            vmem(w_bias.shape[::-1], F32),
            vmem((width, WINDOW), BF16),
            vmem((width, WINDOW), BF16),
            vmem((width, WINDOW), BF16),
            vmem((width, WINDOW), BF16),
            vmem(w_out.shape, BF16),
            vmem(w_down.shape, BF16),
            vmem((EXT, chans), BF16),
            vmem((cols, 1, atoms), jnp.int32),
            vmem((cols, atoms, chans), BF16),
            vmem((atoms, tokens), BF16),
            vmem((tokens, width), F32),
            vmem((tokens, atoms), F32),
            vmem((heads * CHUNK, keys), F32),
            vmem((heads, tokens, keys), BF16),
            vmem((cols, tokens, keys), BF16),
            vmem((width, 3 * LANES), BF16),
            vmem(w_out.shape, BF16),
            vmem((width, tokens), F32),
            vmem((cols, share, LANES), BF16),
            vmem((cols, rows, share, LANES), BF16),
            vmem((cols, head, tokens), BF16),
            sems(13),
            sems(PIECES),
            sems(2),
            sems(2),
            sems(cols),
            sems(cols),
            sems(cols),
            sems(cols),
            sems(cols),
            sems(cols),
            sems(rows),
            sems(rows),
            sems(cols),
            sems(cols),
        ],
        compiler_params=pltpu.CompilerParams(
            collective_id=0, has_side_effects=True, vmem_limit_bytes=56 * 1024 * 1024
        ),
    )(
        atom_feat, atom_token.reshape(1, atoms), w_atom_qkv, w_atom_out, w_atom_up, pair_repr,
        w_bias.T, w_query, w_kv, w_gate, w_out, w_down,
    )
    token_out, atom_final = pl.pallas_call(
        hand_out,
        out_shape=(
            jax.ShapeDtypeStruct((head, tokens), BF16),
            jax.ShapeDtypeStruct((atoms, chans), BF16),
        ),
    )(token_out, atom_final)
    return token_out.T, atom_final


def solution(mesh):
    return jax.shard_map(
        body,
        mesh=mesh,
        in_specs=(
            P(("row", "col"), None),
            P(("row", "col")),
            P(),
            P(),
            P(),
            P("row", None, "col", None),
            P(),
            P(),
            P(),
            P(),
            P(),
            P(),
        ),
        out_specs=(P("row", "col"), P(("row", "col"), None)),
        check_vma=False,
    )
```

```python
import functools

import jax
import jax.numpy as jnp
from jax import lax
from jax.experimental import pallas as pl
from jax.experimental.pallas import tpu as pltpu
from jax.sharding import PartitionSpec as P

MESH = pl.DeviceIdType.MESH
F32 = jnp.float32
BF16 = jnp.bfloat16

EPS = 1e-05
AHEADS = 4
QBLOCK = 32
KWIN = 128
HALO = 48
EXT = 256
CHUNK = 16
PIECES = 8
AHEAD = 2
BEFORE = 1
EARLY = 3
EARLY_SENT = 3
LANES = 128
VOFF = 64
HALVES = 2
ORDER = (10, 9, 11, 8, 6, 5, 7, 4, 14, 13, 15, 12, 2, 1, 3)
NEAR = (1, 3, 2)
WINDOW = 256


def dot(a, b, dims=((1,), (0,))):
    return lax.dot_general(a, b, (dims, ((), ())), preferred_element_type=F32)


def iota(shape, dim):
    return lax.broadcasted_iota(jnp.int32, shape, dim)


def kernel(
    feat, tok, w_qkv, w_ao, w_up, pair, w_bias, w_query, w_kv, w_gate, w_out, w_down,
    out_tok, out_atom,
    xbuf, v_qkv, v_ao, v_up, v_bias, v_q, v_k, v_v, v_g, v_o, v_d,
    ext, tok_all, atoms_all, own_hits, total, count, stage, bias_out, bias_in,
    wsel, w_out_t, act_t, tokens_t, kv_all, g_all,
    load_sem, pair_sem, halo_send, halo_recv, tok_send, tok_recv,
    atom_send, atom_recv, bias_send, bias_recv, kv_send, kv_recv, g_send, g_recv,
):
    rows, cols = lax.axis_size("row"), lax.axis_size("col")
    r, c = lax.axis_index("row"), lax.axis_index("col")
    flat = r * cols + c
    devices = rows * cols
    atoms, chans = feat.shape
    tokens, _, share, _ = pair.shape
    keys = rows * share
    width = w_query.shape[0]
    head = width // cols

    names = ("feat", "tok", "bias", "qkv", "ao", "up", "q", "g", "k", "v", "o", "d")
    part = tokens // PIECES
    first = jnp.minimum(c * head // LANES, (width - WINDOW) // LANES)
    begin = pl.multiple_of(first * LANES, LANES)
    window = pl.ds(begin, WINDOW)
    beside = pl.ds(pl.multiple_of(width + begin, LANES), WINDOW)
    ends = {
        "feat": (feat, ext.at[pl.ds(HALO, atoms)]),
        "tok": (tok, tok_all.at[c]),
        "bias": (w_bias, v_bias),
        "qkv": (w_qkv, v_qkv),
        "ao": (w_ao, v_ao),
        "up": (w_up, v_up),
        "q": (w_query.at[:, window], v_q),
        "g": (w_gate.at[:, window], v_g),
        "k": (w_kv.at[:, window], v_k),
        "v": (w_kv.at[:, beside], v_v),
        "o": (w_out, v_o),
        "d": (w_down, v_d),
    }
    loads = {
        name: pltpu.make_async_copy(*ends[name], load_sem.at[i]) for i, name in enumerate(names)
    }
    pair_loads = [
        pltpu.make_async_copy(
            pair.at[pl.ds(i * part, part)], xbuf.at[pl.ds(i * part, part)], pair_sem.at[i]
        )
        for i in range(PIECES)
    ]
    for name in ("feat", "tok", "bias"):
        loads[name].start()
    for i in range(AHEAD):
        pair_loads[i].start()
    for name in ("qkv", "ao"):
        loads[name].start()

    side = 4
    y, z = c // side, lax.rem(c, side)

    def to(d):
        return lax.rem(y + d % side, side) * side + lax.rem(z + d // side, side)

    def source_of(d):
        return lax.rem(y + side - d % side, side) * side + lax.rem(z + side - d // side, side)

    def col_copy(src, dst, send, recv, d):
        return pltpu.make_async_remote_copy(
            src_ref=src,
            dst_ref=dst,
            send_sem=send.at[d],
            recv_sem=recv.at[d],
            device_id=(r, to(d)),
            device_id_type=MESH,
        )

    barrier = pltpu.get_barrier_semaphore()
    right, left = lax.rem(flat + 1, devices), lax.rem(flat + devices - 1, devices)

    def coords(index):
        return (index // cols, lax.rem(index, cols))

    for peer in (left, right):
        pl.semaphore_signal(barrier, inc=1, device_id=coords(peer), device_id_type=MESH)
    for d in range(1, cols):
        pl.semaphore_signal(
            barrier, inc=1, device_id=(r, lax.rem(c + d, cols)), device_id_type=MESH
        )
    for d in range(1, rows):
        pl.semaphore_signal(
            barrier, inc=1, device_id=(lax.rem(r + d, rows), c), device_id_type=MESH
        )
    ext[pl.ds(atoms + 2 * HALO, EXT - atoms - 2 * HALO), :] = jnp.zeros(
        (EXT - atoms - 2 * HALO, chans), BF16
    )

    loads["bias"].wait()
    wb_t = v_bias[...].astype(BF16)
    wb_sum = jnp.sum(wb_t.astype(F32), axis=1, keepdims=True)
    heads = wb_t.shape[0]
    lhs = jnp.concatenate([wb_t, jnp.ones((16, LANES), BF16)], axis=0)
    ones = jnp.ones((16, LANES), BF16)

    def pair_chunk(index):
        start = pl.multiple_of(index * CHUNK, CHUNK)
        x = xbuf[pl.ds(start, CHUNK)].reshape(CHUNK * keys, LANES)
        x32 = x.astype(F32)
        square = x32 * x32
        high = square.astype(BF16)
        low = (square - high.astype(F32)).astype(BF16)
        proj = dot(lhs, x, ((1,), (1,)))
        squares = dot(ones, high, ((1,), (1,))) + dot(ones, low, ((1,), (1,)))
        mean = proj[heads:heads + 8] * (1.0 / LANES)
        var = squares[:8] * (1.0 / LANES) - mean * mean
        scale = lax.rsqrt(var + EPS)
        mean = jnp.concatenate([mean] * (heads // 8), axis=0)
        scale = jnp.concatenate([scale] * (heads // 8), axis=0)
        bias = (proj[:heads] - mean * wb_sum) * scale
        for q in range(CHUNK):
            stage[pl.ds(q, heads, stride=CHUNK), :] = bias[:, q * keys:(q + 1) * keys]
        for h in range(heads):
            bias_out[h, pl.ds(start, CHUNK), :] = stage[pl.ds(h * CHUNK, CHUNK), :].astype(BF16)

    def bias_copy(i, d):
        span = pl.ds(i * part, part)
        return col_copy(
            bias_out.at[to(d), span], bias_in.at[c, span], bias_send, bias_recv, d
        )

    def pair_piece(i):
        pair_loads[i].wait()
        if i + AHEAD < PIECES:
            pair_loads[i + AHEAD].start()
        steps = part // CHUNK

        def step(k, carry):
            pair_chunk(i * steps + k)
            return carry

        lax.fori_loop(0, steps, step, 0)

    def send_piece(i):
        for d in ORDER:
            bias_copy(i, d).start()

    for i in range(BEFORE):
        pair_piece(i)
    pl.semaphore_wait(barrier, cols + rows)

    to_right = pltpu.make_async_remote_copy(
        src_ref=feat.at[pl.ds(atoms - HALO, HALO)],
        dst_ref=ext.at[pl.ds(0, HALO)],
        send_sem=halo_send.at[0],
        recv_sem=halo_recv.at[0],
        device_id=coords(right),
        device_id_type=MESH,
    )
    to_left = pltpu.make_async_remote_copy(
        src_ref=feat.at[pl.ds(0, HALO)],
        dst_ref=ext.at[pl.ds(HALO + atoms, HALO)],
        send_sem=halo_send.at[1],
        recv_sem=halo_recv.at[1],
        device_id=coords(left),
        device_id_type=MESH,
    )
    to_right.start()
    to_left.start()

    loads["tok"].wait()
    tok_copies = [
        col_copy(tok_all.at[c], tok_all.at[c], tok_send, tok_recv, d) for d in range(1, cols)
    ]
    for copy in tok_copies:
        copy.start()
    for i in range(min(BEFORE, EARLY_SENT)):
        send_piece(i)

    for i in range(BEFORE, EARLY):
        pair_piece(i)
        if i < EARLY_SENT:
            send_piece(i)

    loads["feat"].wait()
    loads["qkv"].wait()
    loads["ao"].wait()
    to_right.wait()
    to_left.wait()
    proj = dot(ext[...], v_qkv[...]).astype(BF16)
    queries = proj[HALO:HALO + atoms, :chans]
    near_keys = proj[:, chans:2 * chans]
    near_vals = proj[:, 2 * chans:]
    lane_head = iota((atoms, chans), 1) // (chans // AHEADS)
    by_head = jnp.concatenate(
        [jnp.where(lane_head == h, queries, jnp.zeros_like(queries)) for h in range(AHEADS)], axis=0
    )
    scores = dot(by_head, near_keys, ((1,), (1,))) * (chans // AHEADS) ** -0.5
    block = lax.rem(iota(scores.shape, 0), atoms) // QBLOCK * QBLOCK
    offset = iota(scores.shape, 1)
    position = flat * atoms + offset - HALO
    valid = (offset >= block) & (offset < block + KWIN)
    valid = valid & (position >= 0) & (position < devices * atoms)
    scores = jnp.where(valid, scores, -1e30)
    expo = jnp.exp(scores - jnp.max(scores, axis=1, keepdims=True))
    denom = jnp.sum(expo, axis=1, keepdims=True)
    mixed = dot(expo.astype(BF16), near_vals) / denom
    context = jnp.zeros((atoms, chans), F32)
    for h in range(AHEADS):
        context = jnp.where(lane_head == h, mixed[h * atoms:(h + 1) * atoms], context)
    atom_out = ext[pl.ds(HALO, atoms), :].astype(F32) + dot(context.astype(BF16), v_ao[...])
    atoms_all[c] = atom_out.astype(BF16)
    atom_copies = [
        col_copy(atoms_all.at[c], atoms_all.at[c], atom_send, atom_recv, d) for d in ORDER
    ]
    for copy in atom_copies:
        copy.start()

    for name in ("up", "q", "g", "k", "v"):
        loads[name].start()
    for i in range(EARLY_SENT, EARLY):
        send_piece(i)
    for copy in tok_copies:
        copy.wait()

    token_of = iota((tokens, atoms), 0) + r * tokens
    arrival = (0,) + ORDER
    group = 4

    def token_group(j):
        cells, hits = [], []
        for d in arrival[j * group:(j + 1) * group]:
            if d:
                atom_copies[ORDER.index(d)].wait()
            slot = source_of(d)
            cells.append(atoms_all[slot])
            hits.append((tok_all[slot] == token_of).astype(F32))
        if j == 0:
            loads["up"].wait()
            own_hits[...] = hits[0].T.astype(BF16)
        up = jnp.maximum(dot(jnp.concatenate(cells, axis=0), v_up[...]), 0.0).astype(BF16)
        added = dot(jnp.concatenate(hits, axis=1).astype(BF16), up)
        counted = sum(hits[1:], hits[0])
        total[...] = added if j == 0 else total[...] + added
        count[...] = counted if j == 0 else count[...] + counted

    for i in range(EARLY, PIECES):
        pair_piece(i)
        send_piece(i)
        if i == PIECES - 3:
            loads["q"].wait()
            loads["g"].wait()
            loads["k"].wait()
            loads["v"].wait()
            source = iota((WINDOW, LANES), 0) - (c * head - begin)
            target = iota((WINDOW, LANES), 1)
            pick = (source == lax.rem(target, VOFF)) & (lax.rem(target, VOFF) < head)
            pick = pick.astype(BF16)
            for k, columns in enumerate((v_q, v_g, v_k, v_v)):
                wsel[:, k * LANES:(k + 1) * LANES] = dot(columns[...], pick).astype(BF16)
        if i >= PIECES - 2:
            token_group(i - PIECES + 2)
    for name in ("o", "d"):
        loads[name].start()
    for j in range(2, cols // group):
        token_group(j)
    act = total[...] * (1.0 / jnp.sum(count[...], axis=1, keepdims=True))
    center = jnp.mean(act, axis=1, keepdims=True)
    spread = jnp.mean(act * act, axis=1, keepdims=True) - center * center
    normed = ((act - center) * lax.rsqrt(spread + EPS)).astype(BF16)
    projected = dot(normed, wsel[...])
    half = tokens // 2
    first_half = iota((half, LANES), 1) < VOFF
    for k in (0, 1):
        part_kv = projected[:, (2 + k) * LANES:(3 + k) * LANES]
        packed = jnp.where(first_half, part_kv[:half], part_kv[half:]).astype(BF16)
        kv_all[k, :, r] = packed.reshape(cols // 2, keys // rows, LANES)
    cores = 2
    x, core = r // cores, lax.rem(r, cores)
    chips = rows // cores

    def chip(dx):
        return lax.rem(x + chips + dx, chips) * cores + core

    def kv_hop(k, dx, over):
        owner, target = (chip(-dx), x * cores + 1 - core) if over else (r, chip(dx))
        return pltpu.make_async_remote_copy(
            src_ref=kv_all.at[k, :, owner],
            dst_ref=kv_all.at[k, :, owner],
            send_sem=kv_send.at[k, dx, over],
            recv_sem=kv_recv.at[k, dx, over],
            device_id=(target, c),
            device_id_type=MESH,
        )

    for k in (0, 1):
        for dx in NEAR:
            kv_hop(k, dx, 0).start()
        kv_hop(k, 0, 1).start()
    low = iota((tokens, LANES), 1) < VOFF
    both_q = projected[:, :LANES].astype(BF16)
    q_low = jnp.where(low, both_q, jnp.zeros_like(both_q))
    q_high = jnp.where(low, jnp.zeros_like(both_q), both_q)
    gate_t = jax.nn.sigmoid(projected[:, LANES:2 * LANES]).T[:head]
    act_t[...] = act.T
    loads["o"].wait()
    w_out_t[...] = v_o[...].T
    bias_in[c] = bias_out[c]

    for k in (0, 1):
        for dx in NEAR:
            kv_hop(k, dx, 0).wait()
            kv_hop(k, dx, 1).start()
    for dx in (0,) + NEAR:
        kv_hop(0, dx, 1).wait()
    for d in range(1, cols):
        col_copy(
            bias_out.at[to(d)], bias_in.at[c], bias_send, bias_recv, d
        ).wait()
    all_keys = kv_all[0].reshape(half * rows, LANES)
    size = tokens // HALVES

    def g_copy(t, d):
        return pltpu.make_async_remote_copy(
            src_ref=g_all.at[t, c],
            dst_ref=g_all.at[t, c],
            send_sem=g_send.at[t, d],
            recv_sem=g_recv.at[t, d],
            device_id=(r, to(d)),
            device_id_type=MESH,
        )

    for t in range(HALVES):
        span = slice(t * size, (t + 1) * size)
        stacked = jnp.concatenate([q_low[span], q_high[span]], axis=0)
        scores = dot(stacked, all_keys, ((1,), (1,))) * head ** -0.5
        bias = jnp.concatenate(
            [
                jnp.concatenate([bias_in[j, span, :] for j in range(k, k + cols // 2)], axis=1)
                for k in (0, cols // 2)
            ],
            axis=0,
        )
        scores = scores + bias.astype(F32)
        top = jnp.max(jnp.maximum(scores[:size], scores[size:]), axis=1, keepdims=True)
        expo = jnp.exp(scores - jnp.concatenate([top, top], axis=0))
        denom = jnp.sum(expo[:size] + expo[size:], axis=1, keepdims=True)
        if t == 0:
            for dx in (0,) + NEAR:
                kv_hop(1, dx, 1).wait()
            all_values = kv_all[1].reshape(half * rows, LANES)
        mixed = dot(expo.astype(BF16), all_values)
        mixed = jnp.where(low[:size], mixed[:size], mixed[size:]) / denom
        mixed = mixed.T
        gated = (mixed[:head] + mixed[VOFF:VOFF + head]) * gate_t[:, span]
        g_all[t, c] = gated.astype(BF16)
        for d in ORDER:
            g_copy(t, d).start()
    loads["d"].wait()
    w_down_t = v_d[...].T
    own_atoms = atoms_all[c].astype(F32)

    final = own_atoms
    for t in range(HALVES):
        span = slice(t * size, (t + 1) * size)
        for d in ORDER:
            g_copy(t, d).wait()
        mixed = dot(w_out_t[...], g_all[t].reshape(width, size))
        token_out = (act_t[:, span] + mixed).astype(BF16)
        token_down = dot(w_down_t, token_out).astype(BF16)
        final = final + dot(own_hits[:, span], token_down, ((1,), (1,)))
        tokens_t[:, span] = token_out
    out_atom[...] = final.astype(BF16)
    out_tok[...] = tokens_t[pl.ds(pl.multiple_of(c * head, head), head), :]


def hand_out(token_in, atom_in, token_out, atom_out):
    token_out[...] = token_in[...]
    atom_out[...] = atom_in[...]


def body(
    atom_feat, atom_token, w_atom_qkv, w_atom_out, w_atom_up, pair_repr, w_bias, w_query, w_kv,
    w_gate, w_out, w_down,
):
    rows, cols = lax.axis_size("row"), lax.axis_size("col")
    atoms, chans = atom_feat.shape
    tokens, _, share, pair_width = pair_repr.shape
    keys = rows * share
    width = w_query.shape[0]
    head = width // cols
    heads = w_bias.shape[1]
    vmem = pltpu.VMEM
    sems = pltpu.SemaphoreType.DMA
    token_out, atom_final = pl.pallas_call(
        kernel,
        out_shape=(
            jax.ShapeDtypeStruct((head, tokens), BF16),
            jax.ShapeDtypeStruct((atoms, chans), BF16),
        ),
        in_specs=[pl.BlockSpec(memory_space=pl.ANY)] * 12,
        out_specs=[pl.BlockSpec(memory_space=pltpu.VMEM)] * 2,
        scratch_shapes=[
            vmem(pair_repr.shape, BF16),
            vmem(w_atom_qkv.shape, BF16),
            vmem(w_atom_out.shape, BF16),
            vmem(w_atom_up.shape, BF16),
            vmem(w_bias.shape[::-1], F32),
            vmem((width, WINDOW), BF16),
            vmem((width, WINDOW), BF16),
            vmem((width, WINDOW), BF16),
            vmem((width, WINDOW), BF16),
            vmem(w_out.shape, BF16),
            vmem(w_down.shape, BF16),
            vmem((EXT, chans), BF16),
            vmem((cols, 1, atoms), jnp.int32),
            vmem((cols, atoms, chans), BF16),
            vmem((atoms, tokens), BF16),
            vmem((tokens, width), F32),
            vmem((tokens, atoms), F32),
            vmem((heads * CHUNK, keys), F32),
            vmem((heads, tokens, keys), BF16),
            vmem((cols, tokens, keys), BF16),
            vmem((width, 4 * LANES), BF16),
            vmem(w_out.shape, BF16),
            vmem((width, tokens), F32),
            vmem((width, tokens), BF16),
            vmem((2, cols // 2, rows, share, LANES), BF16),
            vmem((HALVES, cols, head, tokens // HALVES), BF16),
            sems((13,)),
            sems((PIECES,)),
            sems((2,)),
            sems((2,)),
            sems((cols,)),
            sems((cols,)),
            sems((cols,)),
            sems((cols,)),
            sems((cols,)),
            sems((cols,)),
            sems((2, 4, 2)),
            sems((2, 4, 2)),
            sems((HALVES, cols)),
            sems((HALVES, cols)),
        ],
        compiler_params=pltpu.CompilerParams(
            collective_id=0, has_side_effects=True, vmem_limit_bytes=56 * 1024 * 1024
        ),
    )(
        atom_feat, atom_token.reshape(1, atoms), w_atom_qkv, w_atom_out, w_atom_up, pair_repr,
        w_bias.T, w_query, w_kv, w_gate, w_out, w_down,
    )
    token_out, atom_final = pl.pallas_call(
        hand_out,
        out_shape=(
            jax.ShapeDtypeStruct((head, tokens), BF16),
            jax.ShapeDtypeStruct((atoms, chans), BF16),
        ),
    )(token_out, atom_final)
    return token_out.T, atom_final


def solution(mesh):
    return jax.shard_map(
        body,
        mesh=mesh,
        in_specs=(
            P(("row", "col"), None),
            P(("row", "col")),
            P(),
            P(),
            P(),
            P("row", None, "col", None),
            P(),
            P(),
            P(),
            P(),
            P(),
            P(),
        ),
        out_specs=(P("row", "col"), P(("row", "col"), None)),
        check_vma=False,
    )
```

```python
import functools

import jax
import jax.numpy as jnp
from jax import lax
from jax.experimental import pallas as pl
from jax.experimental.pallas import tpu as pltpu
from jax.sharding import PartitionSpec as P

MESH = pl.DeviceIdType.MESH
F32 = jnp.float32
BF16 = jnp.bfloat16

EPS = 1e-05
AHEADS = 4
QBLOCK = 32
KWIN = 128
HALO = 48
EXT = 256
CHUNK = 16
PIECES = 8
TOGETHER = 2
AHEAD = 2
BEFORE = 1
EARLY = 3
EARLY_SENT = 3
LANES = 128
VOFF = 64
HALVES = 2
ORDER = (10, 9, 11, 8, 6, 5, 7, 4, 14, 13, 15, 12, 2, 1, 3)
NEAR = (1, 3, 2)
WINDOW = 256


def dot(a, b, dims=((1,), (0,))):
    return lax.dot_general(a, b, (dims, ((), ())), preferred_element_type=F32)


def iota(shape, dim):
    return lax.broadcasted_iota(jnp.int32, shape, dim)


def kernel(
    feat, tok, w_qkv, w_ao, w_up, pair, w_bias, w_query, w_kv, w_gate, w_out, w_down,
    out_tok, out_atom,
    xbuf, v_qkv, v_ao, v_up, v_bias, v_q, v_k, v_v, v_g, v_o, v_d,
    ext, tok_all, atoms_all, own_hits, total, count, stage, bias_out, bias_in,
    wsel, w_out_t, act_t, tokens_t, kv_all, g_all,
    load_sem, pair_sem, halo_send, halo_recv, tok_send, tok_recv,
    atom_send, atom_recv, bias_send, bias_recv, kv_send, kv_recv, g_send, g_recv,
):
    rows, cols = lax.axis_size("row"), lax.axis_size("col")
    r, c = lax.axis_index("row"), lax.axis_index("col")
    flat = r * cols + c
    devices = rows * cols
    atoms, chans = feat.shape
    tokens, _, share, _ = pair.shape
    keys = rows * share
    width = w_query.shape[0]
    head = width // cols

    names = ("feat", "tok", "bias", "qkv", "ao", "up", "q", "g", "k", "v", "o", "d")
    part = tokens // PIECES
    first = jnp.minimum(c * head // LANES, (width - WINDOW) // LANES)
    begin = pl.multiple_of(first * LANES, LANES)
    window = pl.ds(begin, WINDOW)
    beside = pl.ds(pl.multiple_of(width + begin, LANES), WINDOW)
    ends = {
        "feat": (feat, ext.at[pl.ds(HALO, atoms)]),
        "tok": (tok, tok_all.at[c]),
        "bias": (w_bias, v_bias),
        "qkv": (w_qkv, v_qkv),
        "ao": (w_ao, v_ao),
        "up": (w_up, v_up),
        "q": (w_query.at[:, window], v_q),
        "g": (w_gate.at[:, window], v_g),
        "k": (w_kv.at[:, window], v_k),
        "v": (w_kv.at[:, beside], v_v),
        "o": (w_out, v_o),
        "d": (w_down, v_d),
    }
    loads = {
        name: pltpu.make_async_copy(*ends[name], load_sem.at[i]) for i, name in enumerate(names)
    }
    pair_loads = [
        pltpu.make_async_copy(
            pair.at[pl.ds(i * part, part)], xbuf.at[pl.ds(i * part, part)], pair_sem.at[i]
        )
        for i in range(PIECES)
    ]
    for name in ("feat", "tok", "bias"):
        loads[name].start()
    for i in range(AHEAD):
        pair_loads[i].start()
    for name in ("qkv", "ao"):
        loads[name].start()

    side = 4
    y, z = c // side, lax.rem(c, side)

    def to(d):
        return lax.rem(y + d % side, side) * side + lax.rem(z + d // side, side)

    def source_of(d):
        return lax.rem(y + side - d % side, side) * side + lax.rem(z + side - d // side, side)

    def col_copy(src, dst, send, recv, d):
        return pltpu.make_async_remote_copy(
            src_ref=src,
            dst_ref=dst,
            send_sem=send.at[d],
            recv_sem=recv.at[d],
            device_id=(r, to(d)),
            device_id_type=MESH,
        )

    barrier = pltpu.get_barrier_semaphore()
    right, left = lax.rem(flat + 1, devices), lax.rem(flat + devices - 1, devices)

    def coords(index):
        return (index // cols, lax.rem(index, cols))

    for peer in (left, right):
        pl.semaphore_signal(barrier, inc=1, device_id=coords(peer), device_id_type=MESH)
    for d in range(1, cols):
        pl.semaphore_signal(
            barrier, inc=1, device_id=(r, lax.rem(c + d, cols)), device_id_type=MESH
        )
    for d in range(1, rows):
        pl.semaphore_signal(
            barrier, inc=1, device_id=(lax.rem(r + d, rows), c), device_id_type=MESH
        )
    ext[pl.ds(atoms + 2 * HALO, EXT - atoms - 2 * HALO), :] = jnp.zeros(
        (EXT - atoms - 2 * HALO, chans), BF16
    )

    loads["bias"].wait()
    wb_t = v_bias[...].astype(BF16)
    wb_sum = jnp.sum(wb_t.astype(F32), axis=1, keepdims=True)
    heads = wb_t.shape[0]
    lhs = jnp.concatenate([wb_t, jnp.ones((16, LANES), BF16)], axis=0)
    ones = jnp.ones((16, LANES), BF16)

    def pair_chunk(index):
        start = pl.multiple_of(index * CHUNK, CHUNK)
        x = xbuf[pl.ds(start, CHUNK)].reshape(CHUNK * keys, LANES)
        x32 = x.astype(F32)
        square = x32 * x32
        high = square.astype(BF16)
        low = (square - high.astype(F32)).astype(BF16)
        proj = dot(lhs, x, ((1,), (1,)))
        squares = dot(ones, high, ((1,), (1,))) + dot(ones, low, ((1,), (1,)))
        mean = proj[heads:heads + 8] * (1.0 / LANES)
        var = squares[:8] * (1.0 / LANES) - mean * mean
        scale = lax.rsqrt(var + EPS)
        mean = jnp.concatenate([mean] * (heads // 8), axis=0)
        scale = jnp.concatenate([scale] * (heads // 8), axis=0)
        bias = (proj[:heads] - mean * wb_sum) * scale
        for q in range(CHUNK):
            stage[pl.ds(q, heads, stride=CHUNK), :] = bias[:, q * keys:(q + 1) * keys]
        for h in range(heads):
            bias_out[h, pl.ds(start, CHUNK), :] = stage[pl.ds(h * CHUNK, CHUNK), :].astype(BF16)

    def bias_copy(i, d):
        span = pl.ds((i + 1 - TOGETHER) * part, TOGETHER * part)
        return col_copy(
            bias_out.at[to(d), span], bias_in.at[c, span], bias_send, bias_recv, d
        )

    def pair_piece(i):
        pair_loads[i].wait()
        if i + AHEAD < PIECES:
            pair_loads[i + AHEAD].start()
        steps = part // CHUNK

        def step(k, carry):
            pair_chunk(i * steps + k)
            return carry

        lax.fori_loop(0, steps, step, 0)

    def send_piece(i):
        if (i + 1) % TOGETHER:
            return
        for d in ORDER:
            bias_copy(i, d).start()

    for i in range(BEFORE):
        pair_piece(i)
    pl.semaphore_wait(barrier, cols + rows)

    to_right = pltpu.make_async_remote_copy(
        src_ref=feat.at[pl.ds(atoms - HALO, HALO)],
        dst_ref=ext.at[pl.ds(0, HALO)],
        send_sem=halo_send.at[0],
        recv_sem=halo_recv.at[0],
        device_id=coords(right),
        device_id_type=MESH,
    )
    to_left = pltpu.make_async_remote_copy(
        src_ref=feat.at[pl.ds(0, HALO)],
        dst_ref=ext.at[pl.ds(HALO + atoms, HALO)],
        send_sem=halo_send.at[1],
        recv_sem=halo_recv.at[1],
        device_id=coords(left),
        device_id_type=MESH,
    )
    to_right.start()
    to_left.start()

    loads["tok"].wait()
    tok_copies = [
        col_copy(tok_all.at[c], tok_all.at[c], tok_send, tok_recv, d) for d in range(1, cols)
    ]
    for copy in tok_copies:
        copy.start()
    for i in range(min(BEFORE, EARLY_SENT)):
        send_piece(i)

    for i in range(BEFORE, EARLY):
        pair_piece(i)
        if i < EARLY_SENT:
            send_piece(i)

    loads["feat"].wait()
    loads["qkv"].wait()
    loads["ao"].wait()
    to_right.wait()
    to_left.wait()
    proj = dot(ext[...], v_qkv[...]).astype(BF16)
    queries = proj[HALO:HALO + atoms, :chans]
    near_keys = proj[:, chans:2 * chans]
    near_vals = proj[:, 2 * chans:]
    lane_head = iota((atoms, chans), 1) // (chans // AHEADS)
    by_head = jnp.concatenate(
        [jnp.where(lane_head == h, queries, jnp.zeros_like(queries)) for h in range(AHEADS)], axis=0
    )
    scores = dot(by_head, near_keys, ((1,), (1,))) * (chans // AHEADS) ** -0.5
    block = lax.rem(iota(scores.shape, 0), atoms) // QBLOCK * QBLOCK
    offset = iota(scores.shape, 1)
    position = flat * atoms + offset - HALO
    valid = (offset >= block) & (offset < block + KWIN)
    valid = valid & (position >= 0) & (position < devices * atoms)
    scores = jnp.where(valid, scores, -1e30)
    expo = jnp.exp(scores - jnp.max(scores, axis=1, keepdims=True))
    denom = jnp.sum(expo, axis=1, keepdims=True)
    mixed = dot(expo.astype(BF16), near_vals) / denom
    context = jnp.zeros((atoms, chans), F32)
    for h in range(AHEADS):
        context = jnp.where(lane_head == h, mixed[h * atoms:(h + 1) * atoms], context)
    atom_out = ext[pl.ds(HALO, atoms), :].astype(F32) + dot(context.astype(BF16), v_ao[...])
    atoms_all[c] = atom_out.astype(BF16)
    atom_copies = [
        col_copy(atoms_all.at[c], atoms_all.at[c], atom_send, atom_recv, d) for d in ORDER
    ]
    for copy in atom_copies:
        copy.start()

    for name in ("up", "q", "g", "k", "v"):
        loads[name].start()
    for i in range(EARLY_SENT, EARLY):
        send_piece(i)
    for copy in tok_copies:
        copy.wait()

    token_of = iota((tokens, atoms), 0) + r * tokens
    arrival = (0,) + ORDER
    group = 4

    def token_group(j):
        cells, hits = [], []
        for d in arrival[j * group:(j + 1) * group]:
            if d:
                atom_copies[ORDER.index(d)].wait()
            slot = source_of(d)
            cells.append(atoms_all[slot])
            hits.append((tok_all[slot] == token_of).astype(F32))
        if j == 0:
            loads["up"].wait()
            own_hits[...] = hits[0].T.astype(BF16)
        up = jnp.maximum(dot(jnp.concatenate(cells, axis=0), v_up[...]), 0.0).astype(BF16)
        added = dot(jnp.concatenate(hits, axis=1).astype(BF16), up)
        counted = sum(hits[1:], hits[0])
        total[...] = added if j == 0 else total[...] + added
        count[...] = counted if j == 0 else count[...] + counted

    for i in range(EARLY, PIECES):
        pair_piece(i)
        send_piece(i)
        if i == PIECES - 3:
            loads["q"].wait()
            loads["g"].wait()
            loads["k"].wait()
            loads["v"].wait()
            source = iota((WINDOW, LANES), 0) - (c * head - begin)
            target = iota((WINDOW, LANES), 1)
            pick = (source == lax.rem(target, VOFF)) & (lax.rem(target, VOFF) < head)
            pick = pick.astype(BF16)
            for k, columns in enumerate((v_q, v_g, v_k, v_v)):
                wsel[:, k * LANES:(k + 1) * LANES] = dot(columns[...], pick).astype(BF16)
        if i >= PIECES - 2:
            token_group(i - PIECES + 2)
    for name in ("o", "d"):
        loads[name].start()
    for j in range(2, cols // group):
        token_group(j)
    act = total[...] * (1.0 / jnp.sum(count[...], axis=1, keepdims=True))
    center = jnp.mean(act, axis=1, keepdims=True)
    spread = jnp.mean(act * act, axis=1, keepdims=True) - center * center
    normed = ((act - center) * lax.rsqrt(spread + EPS)).astype(BF16)
    projected = dot(normed, wsel[...])
    half = tokens // 2
    first_half = iota((half, LANES), 1) < VOFF
    for k in (0, 1):
        part_kv = projected[:, (2 + k) * LANES:(3 + k) * LANES]
        packed = jnp.where(first_half, part_kv[:half], part_kv[half:]).astype(BF16)
        kv_all[k, :, r] = packed.reshape(cols // 2, keys // rows, LANES)
    cores = 2
    x, core = r // cores, lax.rem(r, cores)
    chips = rows // cores

    def chip(dx):
        return lax.rem(x + chips + dx, chips) * cores + core

    def kv_hop(k, dx, over):
        owner, target = (chip(-dx), x * cores + 1 - core) if over else (r, chip(dx))
        return pltpu.make_async_remote_copy(
            src_ref=kv_all.at[k, :, owner],
            dst_ref=kv_all.at[k, :, owner],
            send_sem=kv_send.at[k, dx, over],
            recv_sem=kv_recv.at[k, dx, over],
            device_id=(target, c),
            device_id_type=MESH,
        )

    for k in (0, 1):
        for dx in NEAR:
            kv_hop(k, dx, 0).start()
        kv_hop(k, 0, 1).start()
    low = iota((tokens, LANES), 1) < VOFF
    both_q = projected[:, :LANES].astype(BF16)
    q_low = jnp.where(low, both_q, jnp.zeros_like(both_q))
    q_high = jnp.where(low, jnp.zeros_like(both_q), both_q)
    gate_t = jax.nn.sigmoid(projected[:, LANES:2 * LANES]).T[:head]
    act_t[...] = act.T
    loads["o"].wait()
    w_out_t[...] = v_o[...].T
    bias_in[c] = bias_out[c]

    for k in (0, 1):
        for dx in NEAR:
            kv_hop(k, dx, 0).wait()
            kv_hop(k, dx, 1).start()
    for dx in (0,) + NEAR:
        kv_hop(0, dx, 1).wait()
    for d in range(1, cols):
        col_copy(
            bias_out.at[to(d)], bias_in.at[c], bias_send, bias_recv, d
        ).wait()
    all_keys = kv_all[0].reshape(half * rows, LANES)
    size = tokens // HALVES

    def g_copy(t, d):
        return pltpu.make_async_remote_copy(
            src_ref=g_all.at[t, c],
            dst_ref=g_all.at[t, c],
            send_sem=g_send.at[t, d],
            recv_sem=g_recv.at[t, d],
            device_id=(r, to(d)),
            device_id_type=MESH,
        )

    for t in range(HALVES):
        span = slice(t * size, (t + 1) * size)
        stacked = jnp.concatenate([q_low[span], q_high[span]], axis=0)
        scores = dot(stacked, all_keys, ((1,), (1,))) * head ** -0.5
        bias = jnp.concatenate(
            [
                jnp.concatenate([bias_in[j, span, :] for j in range(k, k + cols // 2)], axis=1)
                for k in (0, cols // 2)
            ],
            axis=0,
        )
        scores = scores + bias.astype(F32)
        top = jnp.max(jnp.maximum(scores[:size], scores[size:]), axis=1, keepdims=True)
        expo = jnp.exp(scores - jnp.concatenate([top, top], axis=0))
        denom = jnp.sum(expo[:size] + expo[size:], axis=1, keepdims=True)
        if t == 0:
            for dx in (0,) + NEAR:
                kv_hop(1, dx, 1).wait()
            all_values = kv_all[1].reshape(half * rows, LANES)
        mixed = dot(expo.astype(BF16), all_values)
        mixed = jnp.where(low[:size], mixed[:size], mixed[size:]) / denom
        mixed = mixed.T
        gated = (mixed[:head] + mixed[VOFF:VOFF + head]) * gate_t[:, span]
        g_all[t, c] = gated.astype(BF16)
        for d in ORDER:
            g_copy(t, d).start()
    loads["d"].wait()
    w_down_t = v_d[...].T
    own_atoms = atoms_all[c].astype(F32)

    final = own_atoms
    for t in range(HALVES):
        span = slice(t * size, (t + 1) * size)
        for d in ORDER:
            g_copy(t, d).wait()
        mixed = dot(w_out_t[...], g_all[t].reshape(width, size))
        token_out = (act_t[:, span] + mixed).astype(BF16)
        token_down = dot(w_down_t, token_out).astype(BF16)
        final = final + dot(own_hits[:, span], token_down, ((1,), (1,)))
        tokens_t[:, span] = token_out
    out_atom[...] = final.astype(BF16)
    out_tok[...] = tokens_t[pl.ds(pl.multiple_of(c * head, head), head), :]


def hand_out(token_in, atom_in, token_out, atom_out):
    token_out[...] = token_in[...]
    atom_out[...] = atom_in[...]


def body(
    atom_feat, atom_token, w_atom_qkv, w_atom_out, w_atom_up, pair_repr, w_bias, w_query, w_kv,
    w_gate, w_out, w_down,
):
    rows, cols = lax.axis_size("row"), lax.axis_size("col")
    atoms, chans = atom_feat.shape
    tokens, _, share, pair_width = pair_repr.shape
    keys = rows * share
    width = w_query.shape[0]
    head = width // cols
    heads = w_bias.shape[1]
    vmem = pltpu.VMEM
    sems = pltpu.SemaphoreType.DMA
    token_out, atom_final = pl.pallas_call(
        kernel,
        out_shape=(
            jax.ShapeDtypeStruct((head, tokens), BF16),
            jax.ShapeDtypeStruct((atoms, chans), BF16),
        ),
        in_specs=[pl.BlockSpec(memory_space=pl.ANY)] * 12,
        out_specs=[pl.BlockSpec(memory_space=pltpu.VMEM)] * 2,
        scratch_shapes=[
            vmem(pair_repr.shape, BF16),
            vmem(w_atom_qkv.shape, BF16),
            vmem(w_atom_out.shape, BF16),
            vmem(w_atom_up.shape, BF16),
            vmem(w_bias.shape[::-1], F32),
            vmem((width, WINDOW), BF16),
            vmem((width, WINDOW), BF16),
            vmem((width, WINDOW), BF16),
            vmem((width, WINDOW), BF16),
            vmem(w_out.shape, BF16),
            vmem(w_down.shape, BF16),
            vmem((EXT, chans), BF16),
            vmem((cols, 1, atoms), jnp.int32),
            vmem((cols, atoms, chans), BF16),
            vmem((atoms, tokens), BF16),
            vmem((tokens, width), F32),
            vmem((tokens, atoms), F32),
            vmem((heads * CHUNK, keys), F32),
            vmem((heads, tokens, keys), BF16),
            vmem((cols, tokens, keys), BF16),
            vmem((width, 4 * LANES), BF16),
            vmem(w_out.shape, BF16),
            vmem((width, tokens), F32),
            vmem((width, tokens), BF16),
            vmem((2, cols // 2, rows, share, LANES), BF16),
            vmem((HALVES, cols, head, tokens // HALVES), BF16),
            sems((13,)),
            sems((PIECES,)),
            sems((2,)),
            sems((2,)),
            sems((cols,)),
            sems((cols,)),
            sems((cols,)),
            sems((cols,)),
            sems((cols,)),
            sems((cols,)),
            sems((2, 4, 2)),
            sems((2, 4, 2)),
            sems((HALVES, cols)),
            sems((HALVES, cols)),
        ],
        compiler_params=pltpu.CompilerParams(
            collective_id=0, has_side_effects=True, vmem_limit_bytes=56 * 1024 * 1024
        ),
    )(
        atom_feat, atom_token.reshape(1, atoms), w_atom_qkv, w_atom_out, w_atom_up, pair_repr,
        w_bias.T, w_query, w_kv, w_gate, w_out, w_down,
    )
    token_out, atom_final = pl.pallas_call(
        hand_out,
        out_shape=(
            jax.ShapeDtypeStruct((head, tokens), BF16),
            jax.ShapeDtypeStruct((atoms, chans), BF16),
        ),
    )(token_out, atom_final)
    return token_out.T, atom_final


def solution(mesh):
    return jax.shard_map(
        body,
        mesh=mesh,
        in_specs=(
            P(("row", "col"), None),
            P(("row", "col")),
            P(),
            P(),
            P(),
            P("row", None, "col", None),
            P(),
            P(),
            P(),
            P(),
            P(),
            P(),
        ),
        out_specs=(P("row", "col"), P(("row", "col"), None)),
        check_vma=False,
    )
```

```python
import functools

import jax
import jax.numpy as jnp
from jax import lax
from jax.experimental import pallas as pl
from jax.experimental.pallas import tpu as pltpu
from jax.sharding import PartitionSpec as P

MESH = pl.DeviceIdType.MESH
F32 = jnp.float32
BF16 = jnp.bfloat16

EPS = 1e-05
AHEADS = 4
QBLOCK = 32
KWIN = 128
HALO = 48
EXT = 256
CHUNK = 16
PIECES = 8
TOGETHER = 2
AHEAD = 2
BEFORE = 1
EARLY = 3
EARLY_SENT = 3
LANES = 128
VOFF = 64
HALVES = 2
ORDER = (10, 9, 11, 8, 6, 5, 7, 4, 14, 13, 15, 12, 2, 1, 3)
NEAR = (1, 3, 2)
WINDOW = 256


def dot(a, b, dims=((1,), (0,))):
    return lax.dot_general(a, b, (dims, ((), ())), preferred_element_type=F32)


def iota(shape, dim):
    return lax.broadcasted_iota(jnp.int32, shape, dim)


def kernel(
    feat, tok, w_qkv, w_ao, w_up, pair, w_bias, w_query, w_kv, w_gate, w_out, w_down,
    out_tok, out_atom,
    xbuf, v_qkv, v_ao, v_up, v_bias, v_q, v_k, v_v, v_g, v_o, v_d,
    ext, tok_all, atoms_all, own_hits, total, count, stage, bias_out, bias_in,
    wsel, w_out_t, act_t, tokens_t, kv_all, g_all,
    load_sem, pair_sem, halo_send, halo_recv, tok_send, tok_recv,
    atom_send, atom_recv, bias_send, bias_recv, kv_send, kv_recv, g_send, g_recv,
):
    rows, cols = lax.axis_size("row"), lax.axis_size("col")
    r, c = lax.axis_index("row"), lax.axis_index("col")
    flat = r * cols + c
    devices = rows * cols
    atoms, chans = feat.shape
    tokens, _, share, _ = pair.shape
    keys = rows * share
    width = w_query.shape[0]
    head = width // cols

    names = ("feat", "tok", "bias", "qkv", "ao", "up", "q", "g", "k", "v", "o", "d")
    part = tokens // PIECES
    first = jnp.minimum(c * head // LANES, (width - WINDOW) // LANES)
    begin = pl.multiple_of(first * LANES, LANES)
    window = pl.ds(begin, WINDOW)
    beside = pl.ds(pl.multiple_of(width + begin, LANES), WINDOW)
    ends = {
        "feat": (feat, ext.at[pl.ds(HALO, atoms)]),
        "tok": (tok, tok_all.at[c]),
        "bias": (w_bias, v_bias),
        "qkv": (w_qkv, v_qkv),
        "ao": (w_ao, v_ao),
        "up": (w_up, v_up),
        "q": (w_query.at[:, window], v_q),
        "g": (w_gate.at[:, window], v_g),
        "k": (w_kv.at[:, window], v_k),
        "v": (w_kv.at[:, beside], v_v),
        "o": (w_out, v_o),
        "d": (w_down, v_d),
    }
    loads = {
        name: pltpu.make_async_copy(*ends[name], load_sem.at[i]) for i, name in enumerate(names)
    }
    pair_loads = [
        pltpu.make_async_copy(
            pair.at[pl.ds(i * part, part)], xbuf.at[pl.ds(i * part, part)], pair_sem.at[i]
        )
        for i in range(PIECES)
    ]
    for name in ("feat", "tok", "bias"):
        loads[name].start()
    for i in range(AHEAD):
        pair_loads[i].start()
    for name in ("qkv", "ao"):
        loads[name].start()

    side = 4
    y, z = c // side, lax.rem(c, side)

    def to(d):
        return lax.rem(y + d % side, side) * side + lax.rem(z + d // side, side)

    def source_of(d):
        return lax.rem(y + side - d % side, side) * side + lax.rem(z + side - d // side, side)

    def col_copy(src, dst, send, recv, d):
        return pltpu.make_async_remote_copy(
            src_ref=src,
            dst_ref=dst,
            send_sem=send.at[d],
            recv_sem=recv.at[d],
            device_id=(r, to(d)),
            device_id_type=MESH,
        )

    barrier = pltpu.get_barrier_semaphore()
    right, left = lax.rem(flat + 1, devices), lax.rem(flat + devices - 1, devices)

    def coords(index):
        return (index // cols, lax.rem(index, cols))

    for peer in (left, right):
        pl.semaphore_signal(barrier, inc=1, device_id=coords(peer), device_id_type=MESH)
    for d in range(1, cols):
        pl.semaphore_signal(
            barrier, inc=1, device_id=(r, lax.rem(c + d, cols)), device_id_type=MESH
        )
    for d in range(1, rows):
        pl.semaphore_signal(
            barrier, inc=1, device_id=(lax.rem(r + d, rows), c), device_id_type=MESH
        )
    ext[pl.ds(atoms + 2 * HALO, EXT - atoms - 2 * HALO), :] = jnp.zeros(
        (EXT - atoms - 2 * HALO, chans), BF16
    )

    loads["bias"].wait()
    wb_t = v_bias[...].astype(BF16)
    wb_sum = jnp.sum(wb_t.astype(F32), axis=1, keepdims=True)
    heads = wb_t.shape[0]
    lhs = jnp.concatenate([wb_t, jnp.ones((16, LANES), BF16)], axis=0)
    ones = jnp.ones((16, LANES), BF16)

    def pair_chunk(index):
        start = pl.multiple_of(index * CHUNK, CHUNK)
        x = xbuf[pl.ds(start, CHUNK)].reshape(CHUNK * keys, LANES)
        x32 = x.astype(F32)
        square = x32 * x32
        high = square.astype(BF16)
        low = (square - high.astype(F32)).astype(BF16)
        proj = dot(lhs, x, ((1,), (1,)))
        squares = dot(ones, high, ((1,), (1,))) + dot(ones, low, ((1,), (1,)))
        mean = proj[heads:heads + 8] * (1.0 / LANES)
        var = squares[:8] * (1.0 / LANES) - mean * mean
        scale = lax.rsqrt(var + EPS)
        mean = jnp.concatenate([mean] * (heads // 8), axis=0)
        scale = jnp.concatenate([scale] * (heads // 8), axis=0)
        bias = (proj[:heads] - mean * wb_sum) * scale
        for q in range(CHUNK):
            stage[pl.ds(q, heads, stride=CHUNK), :] = bias[:, q * keys:(q + 1) * keys]
        for h in range(heads):
            bias_out[h, pl.ds(start, CHUNK), :] = stage[pl.ds(h * CHUNK, CHUNK), :].astype(BF16)

    def bias_copy(i, d):
        span = pl.ds((i + 1 - TOGETHER) * part, TOGETHER * part)
        return col_copy(
            bias_out.at[to(d), span],
            bias_in.at[c, span],
            bias_send.at[i * HALVES // PIECES],
            bias_recv.at[i * HALVES // PIECES],
            d,
        )

    def pair_piece(i):
        pair_loads[i].wait()
        if i + AHEAD < PIECES:
            pair_loads[i + AHEAD].start()
        steps = part // CHUNK

        def step(k, carry):
            pair_chunk(i * steps + k)
            return carry

        lax.fori_loop(0, steps, step, 0)

    def send_piece(i):
        if (i + 1) % TOGETHER:
            return
        for d in ORDER:
            bias_copy(i, d).start()

    for i in range(BEFORE):
        pair_piece(i)
    pl.semaphore_wait(barrier, cols + rows)

    to_right = pltpu.make_async_remote_copy(
        src_ref=feat.at[pl.ds(atoms - HALO, HALO)],
        dst_ref=ext.at[pl.ds(0, HALO)],
        send_sem=halo_send.at[0],
        recv_sem=halo_recv.at[0],
        device_id=coords(right),
        device_id_type=MESH,
    )
    to_left = pltpu.make_async_remote_copy(
        src_ref=feat.at[pl.ds(0, HALO)],
        dst_ref=ext.at[pl.ds(HALO + atoms, HALO)],
        send_sem=halo_send.at[1],
        recv_sem=halo_recv.at[1],
        device_id=coords(left),
        device_id_type=MESH,
    )
    to_right.start()
    to_left.start()

    loads["tok"].wait()
    tok_copies = [
        col_copy(tok_all.at[c], tok_all.at[c], tok_send, tok_recv, d) for d in range(1, cols)
    ]
    for copy in tok_copies:
        copy.start()
    for i in range(min(BEFORE, EARLY_SENT)):
        send_piece(i)

    for i in range(BEFORE, EARLY):
        pair_piece(i)
        if i < EARLY_SENT:
            send_piece(i)

    loads["feat"].wait()
    loads["qkv"].wait()
    loads["ao"].wait()
    to_right.wait()
    to_left.wait()
    proj = dot(ext[...], v_qkv[...]).astype(BF16)
    queries = proj[HALO:HALO + atoms, :chans]
    near_keys = proj[:, chans:2 * chans]
    near_vals = proj[:, 2 * chans:]
    lane_head = iota((atoms, chans), 1) // (chans // AHEADS)
    by_head = jnp.concatenate(
        [jnp.where(lane_head == h, queries, jnp.zeros_like(queries)) for h in range(AHEADS)], axis=0
    )
    scores = dot(by_head, near_keys, ((1,), (1,))) * (chans // AHEADS) ** -0.5
    block = lax.rem(iota(scores.shape, 0), atoms) // QBLOCK * QBLOCK
    offset = iota(scores.shape, 1)
    position = flat * atoms + offset - HALO
    valid = (offset >= block) & (offset < block + KWIN)
    valid = valid & (position >= 0) & (position < devices * atoms)
    scores = jnp.where(valid, scores, -1e30)
    expo = jnp.exp(scores - jnp.max(scores, axis=1, keepdims=True))
    denom = jnp.sum(expo, axis=1, keepdims=True)
    mixed = dot(expo.astype(BF16), near_vals) / denom
    context = jnp.zeros((atoms, chans), F32)
    for h in range(AHEADS):
        context = jnp.where(lane_head == h, mixed[h * atoms:(h + 1) * atoms], context)
    atom_out = ext[pl.ds(HALO, atoms), :].astype(F32) + dot(context.astype(BF16), v_ao[...])
    atoms_all[c] = atom_out.astype(BF16)
    atom_copies = [
        col_copy(atoms_all.at[c], atoms_all.at[c], atom_send, atom_recv, d) for d in ORDER
    ]
    for copy in atom_copies:
        copy.start()

    for name in ("up", "q", "g", "k", "v"):
        loads[name].start()
    for i in range(EARLY_SENT, EARLY):
        send_piece(i)
    for copy in tok_copies:
        copy.wait()

    token_of = iota((tokens, atoms), 0) + r * tokens
    arrival = (0,) + ORDER
    group = 4

    def token_group(j):
        cells, hits = [], []
        for d in arrival[j * group:(j + 1) * group]:
            if d:
                atom_copies[ORDER.index(d)].wait()
            slot = source_of(d)
            cells.append(atoms_all[slot])
            hits.append((tok_all[slot] == token_of).astype(F32))
        if j == 0:
            loads["up"].wait()
            own_hits[...] = hits[0].T.astype(BF16)
        up = jnp.maximum(dot(jnp.concatenate(cells, axis=0), v_up[...]), 0.0).astype(BF16)
        added = dot(jnp.concatenate(hits, axis=1).astype(BF16), up)
        counted = sum(hits[1:], hits[0])
        total[...] = added if j == 0 else total[...] + added
        count[...] = counted if j == 0 else count[...] + counted

    for i in range(EARLY, PIECES):
        pair_piece(i)
        if i < PIECES - 1:
            send_piece(i)
        if i == PIECES - 3:
            loads["q"].wait()
            loads["g"].wait()
            loads["k"].wait()
            loads["v"].wait()
            source = iota((WINDOW, LANES), 0) - (c * head - begin)
            target = iota((WINDOW, LANES), 1)
            pick = (source == lax.rem(target, VOFF)) & (lax.rem(target, VOFF) < head)
            pick = pick.astype(BF16)
            for k, columns in enumerate((v_q, v_g, v_k, v_v)):
                wsel[:, k * LANES:(k + 1) * LANES] = dot(columns[...], pick).astype(BF16)
        if i >= PIECES - 2:
            token_group(i - PIECES + 2)
    for name in ("o", "d"):
        loads[name].start()
    for j in range(2, cols // group):
        token_group(j)
    act = total[...] * (1.0 / jnp.sum(count[...], axis=1, keepdims=True))
    center = jnp.mean(act, axis=1, keepdims=True)
    spread = jnp.mean(act * act, axis=1, keepdims=True) - center * center
    normed = ((act - center) * lax.rsqrt(spread + EPS)).astype(BF16)
    projected = dot(normed, wsel[...])
    half = tokens // 2
    first_half = iota((half, LANES), 1) < VOFF
    for k in (0, 1):
        part_kv = projected[:, (2 + k) * LANES:(3 + k) * LANES]
        packed = jnp.where(first_half, part_kv[:half], part_kv[half:]).astype(BF16)
        kv_all[k, :, r] = packed.reshape(cols // 2, keys // rows, LANES)
    cores = 2
    x, core = r // cores, lax.rem(r, cores)
    chips = rows // cores

    def chip(dx):
        return lax.rem(x + chips + dx, chips) * cores + core

    def kv_hop(k, dx, over):
        owner, target = (chip(-dx), x * cores + 1 - core) if over else (r, chip(dx))
        return pltpu.make_async_remote_copy(
            src_ref=kv_all.at[k, :, owner],
            dst_ref=kv_all.at[k, :, owner],
            send_sem=kv_send.at[k, dx, over],
            recv_sem=kv_recv.at[k, dx, over],
            device_id=(target, c),
            device_id_type=MESH,
        )

    for k in (0, 1):
        for dx in NEAR:
            kv_hop(k, dx, 0).start()
        kv_hop(k, 0, 1).start()
    send_piece(PIECES - 1)
    low = iota((tokens, LANES), 1) < VOFF
    both_q = projected[:, :LANES].astype(BF16)
    q_low = jnp.where(low, both_q, jnp.zeros_like(both_q))
    q_high = jnp.where(low, jnp.zeros_like(both_q), both_q)
    gate_t = jax.nn.sigmoid(projected[:, LANES:2 * LANES]).T[:head]
    act_t[...] = act.T
    loads["o"].wait()
    w_out_t[...] = v_o[...].T
    bias_in[c] = bias_out[c]

    for k in (0, 1):
        for dx in NEAR:
            kv_hop(k, dx, 0).wait()
            kv_hop(k, dx, 1).start()
    for dx in (0,) + NEAR:
        kv_hop(0, dx, 1).wait()
    all_keys = kv_all[0].reshape(half * rows, LANES)
    size = tokens // HALVES

    def g_copy(t, d):
        return pltpu.make_async_remote_copy(
            src_ref=g_all.at[t, c],
            dst_ref=g_all.at[t, c],
            send_sem=g_send.at[t, d],
            recv_sem=g_recv.at[t, d],
            device_id=(r, to(d)),
            device_id_type=MESH,
        )

    for t in range(HALVES):
        span = slice(t * size, (t + 1) * size)
        for d in ORDER:
            col_copy(
                bias_out.at[to(d), pl.ds(t * size, size)],
                bias_in.at[c, pl.ds(t * size, size)],
                bias_send.at[t],
                bias_recv.at[t],
                d,
            ).wait()
        stacked = jnp.concatenate([q_low[span], q_high[span]], axis=0)
        scores = dot(stacked, all_keys, ((1,), (1,))) * head ** -0.5
        bias = jnp.concatenate(
            [
                jnp.concatenate([bias_in[j, span, :] for j in range(k, k + cols // 2)], axis=1)
                for k in (0, cols // 2)
            ],
            axis=0,
        )
        scores = scores + bias.astype(F32)
        top = jnp.max(jnp.maximum(scores[:size], scores[size:]), axis=1, keepdims=True)
        expo = jnp.exp(scores - jnp.concatenate([top, top], axis=0))
        denom = jnp.sum(expo[:size] + expo[size:], axis=1, keepdims=True)
        if t == 0:
            for dx in (0,) + NEAR:
                kv_hop(1, dx, 1).wait()
            all_values = kv_all[1].reshape(half * rows, LANES)
        mixed = dot(expo.astype(BF16), all_values)
        mixed = jnp.where(low[:size], mixed[:size], mixed[size:]) / denom
        mixed = mixed.T
        gated = (mixed[:head] + mixed[VOFF:VOFF + head]) * gate_t[:, span]
        g_all[t, c] = gated.astype(BF16)
        for d in ORDER:
            g_copy(t, d).start()
    loads["d"].wait()
    w_down_t = v_d[...].T
    own_atoms = atoms_all[c].astype(F32)

    final = own_atoms
    for t in range(HALVES):
        span = slice(t * size, (t + 1) * size)
        for d in ORDER:
            g_copy(t, d).wait()
        mixed = dot(w_out_t[...], g_all[t].reshape(width, size))
        token_out = (act_t[:, span] + mixed).astype(BF16)
        token_down = dot(w_down_t, token_out).astype(BF16)
        final = final + dot(own_hits[:, span], token_down, ((1,), (1,)))
        tokens_t[:, span] = token_out
    out_atom[...] = final.astype(BF16)
    out_tok[...] = tokens_t[pl.ds(pl.multiple_of(c * head, head), head), :]


def hand_out(token_in, atom_in, token_out, atom_out):
    token_out[...] = token_in[...]
    atom_out[...] = atom_in[...]


def body(
    atom_feat, atom_token, w_atom_qkv, w_atom_out, w_atom_up, pair_repr, w_bias, w_query, w_kv,
    w_gate, w_out, w_down,
):
    rows, cols = lax.axis_size("row"), lax.axis_size("col")
    atoms, chans = atom_feat.shape
    tokens, _, share, pair_width = pair_repr.shape
    keys = rows * share
    width = w_query.shape[0]
    head = width // cols
    heads = w_bias.shape[1]
    vmem = pltpu.VMEM
    sems = pltpu.SemaphoreType.DMA
    token_out, atom_final = pl.pallas_call(
        kernel,
        out_shape=(
            jax.ShapeDtypeStruct((head, tokens), BF16),
            jax.ShapeDtypeStruct((atoms, chans), BF16),
        ),
        in_specs=[pl.BlockSpec(memory_space=pl.ANY)] * 12,
        out_specs=[pl.BlockSpec(memory_space=pltpu.VMEM)] * 2,
        scratch_shapes=[
            vmem(pair_repr.shape, BF16),
            vmem(w_atom_qkv.shape, BF16),
            vmem(w_atom_out.shape, BF16),
            vmem(w_atom_up.shape, BF16),
            vmem(w_bias.shape[::-1], F32),
            vmem((width, WINDOW), BF16),
            vmem((width, WINDOW), BF16),
            vmem((width, WINDOW), BF16),
            vmem((width, WINDOW), BF16),
            vmem(w_out.shape, BF16),
            vmem(w_down.shape, BF16),
            vmem((EXT, chans), BF16),
            vmem((cols, 1, atoms), jnp.int32),
            vmem((cols, atoms, chans), BF16),
            vmem((atoms, tokens), BF16),
            vmem((tokens, width), F32),
            vmem((tokens, atoms), F32),
            vmem((heads * CHUNK, keys), F32),
            vmem((heads, tokens, keys), BF16),
            vmem((cols, tokens, keys), BF16),
            vmem((width, 4 * LANES), BF16),
            vmem(w_out.shape, BF16),
            vmem((width, tokens), F32),
            vmem((width, tokens), BF16),
            vmem((2, cols // 2, rows, share, LANES), BF16),
            vmem((HALVES, cols, head, tokens // HALVES), BF16),
            sems((13,)),
            sems((PIECES,)),
            sems((2,)),
            sems((2,)),
            sems((cols,)),
            sems((cols,)),
            sems((cols,)),
            sems((cols,)),
            sems((HALVES, cols)),
            sems((HALVES, cols)),
            sems((2, 4, 2)),
            sems((2, 4, 2)),
            sems((HALVES, cols)),
            sems((HALVES, cols)),
        ],
        compiler_params=pltpu.CompilerParams(
            collective_id=0, has_side_effects=True, vmem_limit_bytes=56 * 1024 * 1024
        ),
    )(
        atom_feat, atom_token.reshape(1, atoms), w_atom_qkv, w_atom_out, w_atom_up, pair_repr,
        w_bias.T, w_query, w_kv, w_gate, w_out, w_down,
    )
    token_out, atom_final = pl.pallas_call(
        hand_out,
        out_shape=(
            jax.ShapeDtypeStruct((head, tokens), BF16),
            jax.ShapeDtypeStruct((atoms, chans), BF16),
        ),
    )(token_out, atom_final)
    return token_out.T, atom_final


def solution(mesh):
    return jax.shard_map(
        body,
        mesh=mesh,
        in_specs=(
            P(("row", "col"), None),
            P(("row", "col")),
            P(),
            P(),
            P(),
            P("row", None, "col", None),
            P(),
            P(),
            P(),
            P(),
            P(),
            P(),
        ),
        out_specs=(P("row", "col"), P(("row", "col"), None)),
        check_vma=False,
    )
```
